256 devices in a mesh: ctx: 8 (over z), expert: 32 (over y, x, core).
Axes of the slice: x: 4, y: 4, z: 8, core: 2. Of those that a mesh axis runs over, the one named last changes fastest.
Arguments:
- tokens: bfloat16 [32, 1024, 1024], P('expert', 'ctx'), may hold values from -6 to 6
- chain_ids: int32 [32, 1024], P('expert', 'ctx'), may hold values from 0 to 7, never falling along the last dimension, each value on 1 to 256 neighbouring positions
- route_ids: int32 [32, 1024, 6], P('expert', 'ctx'), may hold values from 0 to 31, all different within a row; in each aligned block of 128 rows (0 to 127, 128 to 255, ..., all dimensions but the last counted through in order) at most 32 rows name the same one
- route_weights: float32 [32, 1024, 6], P('expert', 'ctx'), may hold values from 0.1 to 0.5
- attn_gain: float32 [1024], replicated, may hold values from 0.6 to 12
- ffn_gain: float32 [1024], replicated, may hold values from 0.1 to 1.9
- chain_bias: float32 [8], replicated, may hold values from 0.5 to 2.5
- w_qkv: bfloat16 [3, 1024, 1024], P(None, 'expert', 'ctx'), may hold values from -0.1875 to 0.1875
- w_out: bfloat16 [1024, 1024], P('ctx', 'expert'), may hold values from -0.75 to 0.75
- w_gateup: bfloat16 [32, 1024, 2816], P('expert'), may hold values from -0.1875 to 0.1875
- w_down: bfloat16 [32, 1408, 1024], P('expert'), may hold values from -0.15625 to 0.15625
Outputs:
- layer_out: bfloat16 [32, 1024, 1024], P('expert', 'ctx')
The draws below stay inside these ranges and needn't reach their ends.
Inputs may be any that keep to these rules, and one draw needn't show every extreme that they name: `route_ids`: each residue names 6 different experts. Among the 128 residues of one device (aligned blocks of the residues in order, crop after crop), no expert is named by more than 32 of them, and in every draw some expert is named by exactly 32. `chain_ids`: chain numbers never fall along a crop; a chain spans 1 to 256 residues, and some chain exactly that many.
All inputs are finite; a program needn't handle non-finite values.
Results may differ from the reference program's by a relative error of at most 0.02.
The reference program's roundings to bfloat16 on the way count: a program that leaves them out, or rounds other values in their place, can miss the bound.
Values may be sent and summed in bfloat16 or wider, within the bound.
No kernel may reach another device: no remote copies, remote signals or barrier semaphores. Data moves between devices by JAX's collectives and lax.ppermute only.
A program may use at most 64 MiB of HBM per device.

```python
import math
import jax
import jax.numpy as jnp
import numpy as np
from jax import lax

D = 1024
HEADS = 8
FF = 1408
EXPERTS = 32
TOPK = 6
CHAINS = 8
TOK_DEV = 128
CROP_LEN = 1024
CROPS = 32
CAP = 32


def draw_attn_gain(key, part):
    return jax.random.uniform(key, (D,), jnp.float32, 0.6, 1.4)


def block_scale(key, dims, split, least, high):
    factor_of = 1.0
    for position, shards_of in split:
        heights = jax.random.uniform(jax.random.fold_in(jax.random.fold_in(key, 6), position), (shards_of,), jnp.float32, least / len(split), high / len(split))
        factor_of = factor_of * jnp.repeat(jnp.exp(heights), dims[position] // shards_of).reshape((-1,) + (1,) * (len(dims) - 1 - position))
    return factor_of


def split_up(count, total, bound, skew):
    weights = [(1 << 20) // math.isqrt(grade ** skew) + 1 for grade in range(2, count + 1)]
    spare, counts = total - bound - (count - 1), [1] * (count - 1)
    while spare > 0:
        free = [i for i in range(count - 1) if counts[i] < bound]
        whole, budget = sum([weights[i] for i in free]), spare
        for i in free:
            addition = min(bound - counts[i], max(1, budget * weights[i] // whole), spare)
            counts[i] = counts[i] + addition
            spare = spare - addition
    return np.array([bound] + counts)


def uneven(key, amount, total, reach, slope):
    if amount == 2:
        one = jax.random.randint(key, (), max(1, total - reach), min(reach, total - 1) + 1)
        return jnp.stack([one, total - one])
    lengths = jnp.asarray(split_up(amount, total, reach, slope), jnp.int32)
    couples = (amount - 1) // 2
    donor, sink = lengths[1:1 + 2 * couples:2], lengths[2:2 + 2 * couples:2]
    room = jnp.minimum(donor - 1, reach - sink)
    shifted = jax.random.randint(jax.random.fold_in(key, 1), (couples,), 0, 1 << 20) % (room + 1)
    lengths = lengths.at[1:1 + 2 * couples:2].set(donor - shifted).at[2:2 + 2 * couples:2].set(sink + shifted)
    return lengths[jax.random.permutation(jax.random.fold_in(key, 2), amount)]


def deal_out(own_key, own, number, rows, amount, top, most, lean):
    ranking = jax.random.permutation(own_key, amount)
    crowded, usual = shares(amount, rows * top, most, lean, True), shares(amount, rows * top, most, lean, False)
    places = jnp.arange(amount)

    def named(lengths, offset_by):
        used = int((lengths > 0).sum())
        fixed = max(1, used // 4)
        passed = fixed + (places - fixed + offset_by * (used - fixed)) % max(1, amount - fixed)
        return jnp.zeros((amount,), jnp.int32).at[ranking[jnp.where(places < fixed, places, passed)]].set(jnp.asarray(lengths, jnp.int32))

    lengths = jnp.where(number % 4 == 0, named(crowded, number // 4), named(usual, number - number // 4 - 1))
    mixed = jax.random.permutation(jax.random.fold_in(own, 3), amount)
    source_of, taker = mixed[0:amount // 2 * 2:2], mixed[1:amount // 2 * 2:2]
    room = jnp.minimum(lengths[source_of] - 1, most - lengths[taker]) // 2
    room = jnp.where((source_of == ranking[0]) | (taker == ranking[0]) | (lengths[taker] == 0), 0, jnp.maximum(room, 0))
    passed = jax.random.randint(jax.random.fold_in(own, 4), (amount // 2,), 0, 1 << 20) % (room + 1)
    lengths = lengths.at[source_of].add(-passed).at[taker].add(passed)
    labels = jnp.searchsorted(jnp.cumsum(lengths), jnp.arange(rows * top), side="right").astype(jnp.int32)
    table = labels.reshape(top, rows).T
    table = table[jax.random.permutation(jax.random.fold_in(own, 1), rows)]
    offset_by = jax.random.randint(jax.random.fold_in(own, 2), (rows, 1), 0, top)
    return jnp.take_along_axis(table, (jnp.arange(top)[None, :] + offset_by) % top, axis=1)


def shares(amount, total, reach, lean, full):
    weights = [(1 << 20) // math.isqrt(grade ** lean) + 1 for grade in range(1, amount + 1)]
    largest = reach if full else min(reach, max(-(-total // amount), total * weights[0] // sum(weights)))
    least = 1 if total - largest >= amount - 1 else 0
    counts, rest = [largest] + [least] * (amount - 1), total - largest - least * (amount - 1)
    while rest > 0:
        free = [i for i in range(1, amount) if counts[i] < largest] or [i for i in range(1, amount) if counts[i] < reach]
        pool, budget = sum([weights[i] for i in free]), rest
        for i in free:
            extra = min(reach - counts[i], max(1, budget * weights[i] // pool), rest)
            counts[i] = counts[i] + extra
            rest = rest - extra
    return np.array(counts)


def scatter_about(own_key, extent, spread, reach, cuts=(), kind=jnp.bfloat16):
    values = jax.random.normal(own_key, extent, jnp.float32) * spread
    if len(cuts) > 0:
        values = block_scale(own_key, extent, cuts, -0.22, 0.18) * values
    return jnp.clip(values, min=-reach, max=reach).astype(kind)


def setup_inputs(seed: int = 0) -> dict:
    arg_keys = jax.random.split(jax.random.key(seed), 12)
    tokens = scatter_about(arg_keys[0], (CROPS, CROP_LEN, D), 1.0, 6.0, ((0, 32), (1, 8)))
    chain_ids = jax.vmap(lambda own: jnp.searchsorted(jnp.cumsum(uneven(own, CHAINS, CROP_LEN, CROP_LEN // 4, 0)), jnp.arange(CROP_LEN), side="right"))(jax.random.split(arg_keys[1], CROPS)).reshape((CROPS, CROP_LEN)).astype(jnp.int32)
    route_ids_keys = jax.random.split(jax.random.fold_in(arg_keys[2], 1), CROPS * CROP_LEN // TOK_DEV)
    route_ids_turns = jax.random.permutation(jax.random.fold_in(arg_keys[2], 3), CROPS * CROP_LEN // TOK_DEV)
    route_ids = jax.vmap(lambda own, number: deal_out(jax.random.fold_in(arg_keys[2], 2), own, number, TOK_DEV, EXPERTS, TOPK, CAP, 2))(route_ids_keys, route_ids_turns).reshape((CROPS, CROP_LEN, TOPK))
    route_weights = jnp.clip(0.1 + 0.4 * jax.random.uniform(arg_keys[3], (CROPS, CROP_LEN, TOPK), jnp.float32) ** block_scale(arg_keys[3], (CROPS, CROP_LEN, TOPK), ((0, 32), (1, 8)), -0.2, 0.2), 0.1, 0.5)
    attn_gain = draw_attn_gain(jax.random.fold_in(arg_keys[11], 71), 0)
    ffn_gain = jnp.clip(1.0 + 0.18 * jax.random.normal(arg_keys[5], (D,), jnp.float32), 0.1, 1.9)
    chain_bias = jnp.clip(jax.random.uniform(arg_keys[6], (HEADS,), jnp.float32, 0.5, 2.5), 0.5, 2.5)
    w_qkv = scatter_about(arg_keys[7], (3, D, D), D ** -0.5, 0.1875, ((1, 32), (2, 8)))
    w_out = scatter_about(arg_keys[8], (D, D), (D // 16) ** -0.5, 0.75, ((0, 8), (1, 32)))
    w_gateup = scatter_about(arg_keys[9], (EXPERTS, D, 2 * FF), D ** -0.5, 0.1875, ((0, 32),))
    w_down = scatter_about(arg_keys[10], (EXPERTS, FF, D), FF ** -0.5, 0.15625, ((0, 32),))
    return dict(tokens=tokens, chain_ids=chain_ids, route_ids=route_ids, route_weights=route_weights, attn_gain=attn_gain, ffn_gain=ffn_gain, chain_bias=chain_bias, w_qkv=w_qkv, w_out=w_out, w_gateup=w_gateup, w_down=w_down)


def rms_scale(values, gain):
    wide = values.astype(jnp.float32)
    return wide * lax.rsqrt(lax.optimization_barrier(jnp.mean(wide * wide, axis=-1, keepdims=True)) + 1e-05) * gain

def reference(tokens, chain_ids, route_ids, route_weights, attn_gain, ffn_gain, chain_bias, w_qkv, w_out, w_gateup, w_down):
    crops, length, width = tokens.shape
    heads = HEADS
    head_dim = width // heads
    scale = 1.0 / math.sqrt(head_dim)
    normed = rms_scale(tokens, attn_gain).astype(jnp.bfloat16).reshape(crops * length, width)
    query = jnp.dot(normed, w_qkv[0], preferred_element_type=jnp.float32).astype(jnp.bfloat16).reshape(crops, length, heads, head_dim)
    key = jnp.dot(normed, w_qkv[1], preferred_element_type=jnp.float32).astype(jnp.bfloat16).reshape(crops, length, heads, head_dim)
    value = jnp.dot(normed, w_qkv[2], preferred_element_type=jnp.float32).astype(jnp.bfloat16).reshape(crops, length, heads, head_dim)

    def one_crop(items):
        q_crop, k_crop, v_crop, c_crop = items
        scores = jnp.einsum('qhd,khd->hqk', q_crop.astype(jnp.float32), k_crop.astype(jnp.float32)) * scale
        same = (c_crop[:, None] == c_crop[None, :]).astype(jnp.float32)
        scores = scores + chain_bias[:, None, None] * same[None]
        top = lax.optimization_barrier(jnp.max(scores, axis=-1, keepdims=True))
        raised = jnp.exp(scores - top)
        probs = (raised / lax.optimization_barrier(jnp.sum(raised, axis=-1, keepdims=True))).astype(jnp.bfloat16)
        mixed_crop = jnp.einsum('hqk,khd->qhd', probs.astype(jnp.float32), v_crop.astype(jnp.float32))
        return mixed_crop.astype(jnp.bfloat16).reshape(length, width)
    attended = lax.map(one_crop, (query, key, value, chain_ids)).reshape(crops * length, width)
    mixed = tokens.reshape(crops * length, width).astype(jnp.float32) + jnp.dot(attended, w_out, preferred_element_type=jnp.float32)
    ffn_in = rms_scale(mixed, ffn_gain).astype(jnp.bfloat16)
    tok_dev = TOK_DEV
    topk = TOPK
    experts = EXPERTS
    cap = CAP
    ff = FF
    blocks = crops * length // tok_dev
    ids = route_ids.reshape(blocks, tok_dev * topk)
    onehot = (ids[:, :, None] == jnp.arange(experts, dtype=jnp.int32)[None, None, :]).astype(jnp.int32)
    rank = lax.optimization_barrier(jnp.sum((jnp.cumsum(onehot, axis=1) - onehot) * onehot, axis=2))
    slots = (ids * cap + rank).astype(jnp.int32)
    token_index = (jnp.arange(blocks, dtype=jnp.int32)[:, None] * tok_dev + jnp.arange(tok_dev * topk, dtype=jnp.int32)[None, :] // topk).astype(jnp.int32)
    block_index = jnp.broadcast_to(jnp.arange(blocks, dtype=jnp.int32)[:, None], slots.shape)
    source = jnp.zeros((blocks, experts * cap), jnp.int32).at[block_index, slots].set(token_index)
    weight_table = jnp.zeros((blocks, experts * cap), jnp.float32).at[block_index, slots].set(route_weights.reshape(blocks, tok_dev * topk).astype(jnp.float32))

    def expert_step(total, expert):
        start = (expert * cap).astype(jnp.int32)
        index = lax.dynamic_slice_in_dim(source, start, cap, 1).reshape(-1)
        weight = lax.dynamic_slice_in_dim(weight_table, start, cap, 1).reshape(-1)
        rows = jnp.take(ffn_in, index, axis=0)
        both = jnp.dot(rows, w_gateup[expert], preferred_element_type=jnp.float32)
        active = (jax.nn.silu(both[:, :ff]) * both[:, ff:]).astype(jnp.bfloat16)
        result = jnp.dot(active, w_down[expert], preferred_element_type=jnp.float32).astype(jnp.bfloat16)
        total = total.at[index].add(weight[:, None] * result.astype(jnp.float32))
        return (total, None)
    moe_sum, _ = lax.scan(expert_step, jnp.zeros((crops * length, width), jnp.float32), jnp.arange(experts, dtype=jnp.int32))
    return (mixed + moe_sum).astype(jnp.bfloat16).reshape(crops, length, width)
```

```python
import functools
import math

import jax
import jax.numpy as jnp
from jax import lax
from jax.experimental import pallas as pl
from jax.experimental.pallas import tpu as pltpu
from jax.sharding import PartitionSpec as P

F32 = jnp.float32
BF16 = jnp.bfloat16
MIB = 1 << 20
CHUNKS = 1
CAP = 32


def vmem_spec():
    return pl.BlockSpec(memory_space=pltpu.VMEM)


def smem_spec():
    return pl.BlockSpec(memory_space=pltpu.SMEM)


def rms_scale(values, gain):
    wide = values.astype(F32)
    return wide * lax.rsqrt(jnp.mean(wide * wide, axis=-1, keepdims=True) + 1e-05) * gain


def slot_parts(shape, dim, experts, cap):
    slot = lax.broadcasted_iota(jnp.int32, shape, dim)
    part = cap // CHUNKS
    per_chunk = experts * part
    within = lax.rem(slot, per_chunk)
    return within // part, (slot // per_chunk) * part + lax.rem(within, part)


def route_kernel(experts, cap, ids_ref, idst_ref, weights_ref, pick_ref, high_ref, low_ref):
    tok, topk = ids_ref.shape
    slots = experts * cap
    named = jnp.zeros((tok, experts), F32)
    gates = jnp.zeros((tok, experts), F32)
    lane = lax.broadcasted_iota(jnp.int32, (tok, experts), 1)
    for route in range(topk):
        hit = ids_ref[:, route : route + 1] == lane
        named = named + jnp.where(hit, 1.0, 0.0)
        gates = gates + jnp.where(hit, weights_ref[:, route : route + 1], 0.0)
    row = lax.broadcasted_iota(jnp.int32, (tok, tok), 0)
    col = lax.broadcasted_iota(jnp.int32, (tok, tok), 1)
    before = jnp.where(col < row, 1.0, 0.0).astype(BF16)
    named16 = named.astype(BF16)
    rank = jnp.dot(before, named16, preferred_element_type=F32)
    expert_of, place_of = slot_parts((experts, slots), 1, experts, cap)
    spread = jnp.where(
        lax.broadcasted_iota(jnp.int32, (experts, slots), 0) == expert_of, 1.0, 0.0
    ).astype(BF16)
    place = place_of[0:1, :].astype(F32)
    mine = jnp.where(named > 0.5, rank, -1.0).astype(BF16)
    here = jnp.dot(mine, spread, preferred_element_type=F32) == place
    high = gates.astype(BF16)
    low = (gates - high.astype(F32)).astype(BF16)
    high_ref[...] = jnp.where(
        here, jnp.dot(high, spread, preferred_element_type=F32), 0.0
    ).astype(BF16)
    low_ref[...] = jnp.where(
        here, jnp.dot(low, spread, preferred_element_type=F32), 0.0
    ).astype(BF16)

    named_t = jnp.zeros((experts, tok), F32)
    sub = lax.broadcasted_iota(jnp.int32, (experts, tok), 0)
    for route in range(topk):
        named_t = named_t + jnp.where(idst_ref[route : route + 1, :] == sub, 1.0, 0.0)
    after = jnp.where(row < col, 1.0, 0.0).astype(BF16)
    rank_t = jnp.dot(named_t.astype(BF16), after, preferred_element_type=F32)
    mine_t = jnp.where(named_t > 0.5, rank_t, -1.0).astype(BF16)
    expert_t, place_t = slot_parts((slots, experts), 0, experts, cap)
    spread_t = jnp.where(
        lax.broadcasted_iota(jnp.int32, (slots, experts), 1) == expert_t, 1.0, 0.0
    ).astype(BF16)
    here_t = jnp.dot(spread_t, mine_t, preferred_element_type=F32) == place_t[:, 0:1].astype(F32)
    pick_ref[...] = jnp.where(here_t, 1.0, 0.0).astype(BF16)


def route_tables(ids, weights, experts, cap):
    tok, topk = ids.shape
    slots = experts * cap
    return pl.pallas_call(
        functools.partial(route_kernel, experts, cap),
        out_shape=[
            jax.ShapeDtypeStruct((slots, tok), BF16),
            jax.ShapeDtypeStruct((tok, slots), BF16),
            jax.ShapeDtypeStruct((tok, slots), BF16),
        ],
        in_specs=[vmem_spec()] * 3,
        out_specs=[vmem_spec()] * 3,
        compiler_params=pltpu.CompilerParams(vmem_limit_bytes=8 * MIB),
        cost_estimate=pl.CostEstimate(flops=2 * 10**8, bytes_accessed=10**6, transcendentals=0),
        name="route_tables",
    )(ids, ids.T, weights)


def attention_kernel(
    steps, me_ref, bias_ref, chain_ref, w_ref, *refs
):
    blocks, (out_ref, w_buf, q_buf, k_buf, v_buf) = refs[:-5], refs[-5:]
    me = me_ref[0]
    ring = len(steps)
    tok = out_ref.shape[1]
    head_dim = out_ref.shape[2]
    width = w_buf.shape[0]
    for i in range(3):
        w_buf[:, i * head_dim : (i + 1) * head_dim] = w_ref[:, i].reshape(width, head_dim)
    start = 0
    for block in blocks:
        rows = block.shape[0]
        both = jnp.dot(block[...], w_buf[...], preferred_element_type=F32).astype(BF16)
        q_buf[start : start + rows] = both[:, :head_dim]
        k_buf[start : start + rows] = both[:, head_dim : 2 * head_dim]
        v_buf[start : start + rows] = both[:, 2 * head_dim :]
        start += rows
    owner = [lax.rem(me + (s + ring), ring) for s in steps]
    rows_of = [chain_ref[o] for o in owner]
    key_chain = jnp.concatenate(rows_of, axis=1)
    scale = 1.0 / math.sqrt(head_dim)
    bias = bias_ref[me]
    pair = 2
    for first in range(0, ring, pair):
        query_chain = jnp.concatenate(
            [
                jnp.broadcast_to(rows_of[first + j], (tok, tok)).T
                for j in range(pair)
            ],
            axis=0,
        )
        query_chain = jnp.concatenate([query_chain] * ring, axis=1)
        query = q_buf[first * tok : (first + pair) * tok]
        scores = (
            lax.dot_general(
                query, k_buf[...], (((1,), (1,)), ((), ())), preferred_element_type=F32
            )
            * scale
        )
        scores = scores + jnp.where(query_chain == key_chain, bias, 0.0)
        top = jnp.max(scores, axis=-1, keepdims=True)
        raised = jnp.exp(scores - top)
        probs = (raised * (1.0 / jnp.sum(raised, axis=-1, keepdims=True))).astype(BF16)
        mixed = jnp.dot(probs, v_buf[...], preferred_element_type=F32).astype(BF16)
        for j in range(pair):
            out_ref[owner[first + j]] = mixed[j * tok : (j + 1) * tok]


def attention(me, bias, chains, weights, blocks, steps):
    ring = len(steps)
    tok = chains.shape[2]
    head_dim = weights.shape[3]
    width = weights.shape[0] * weights.shape[2]
    length = ring * tok
    return pl.pallas_call(
        functools.partial(attention_kernel, steps),
        out_shape=jax.ShapeDtypeStruct((ring, tok, head_dim), BF16),
        in_specs=[smem_spec(), smem_spec()] + [vmem_spec()] * (2 + len(blocks)),
        out_specs=vmem_spec(),
        scratch_shapes=[
            pltpu.VMEM((width, 3 * head_dim), BF16),
            pltpu.VMEM((length, head_dim), BF16),
            pltpu.VMEM((length, head_dim), BF16),
            pltpu.VMEM((length, head_dim), BF16),
        ],
        compiler_params=pltpu.CompilerParams(vmem_limit_bytes=24 * MIB),
        cost_estimate=pl.CostEstimate(
            flops=1400 * 10**6, bytes_accessed=3 * 10**6, transcendentals=10**6
        ),
        name="attention",
    )(me, bias, chains, weights, *blocks)


def dispatch_kernel(heads_ref, w_ref, tokens_ref, gain_ref, pick_ref, mixed_ref, *out_refs):
    local = jnp.concatenate([heads_ref[h] for h in range(heads_ref.shape[0])], axis=1)
    mixed = tokens_ref[...].astype(F32) + lax.dot_general(
        local, w_ref[...], (((1,), (1,)), ((), ())), preferred_element_type=F32
    )
    mixed_ref[...] = mixed
    ffn_in = (
        mixed * lax.rsqrt(jnp.mean(mixed * mixed, axis=-1, keepdims=True) + 1e-05) * gain_ref[...]
    ).astype(BF16)
    start = 0
    for ref in out_refs:
        experts, rows, width = ref.shape
        count = experts * rows
        ref[...] = (
            jnp.dot(pick_ref[start : start + count], ffn_in, preferred_element_type=F32)
            .astype(BF16)
            .reshape(experts, rows, width)
        )
        start += count


def dispatch(heads, w_out, tokens, gain, pick, experts, cap):
    tok, width = tokens.shape
    return pl.pallas_call(
        dispatch_kernel,
        out_shape=[jax.ShapeDtypeStruct((tok, width), F32)]
        + [jax.ShapeDtypeStruct((experts, cap // CHUNKS, width), BF16)] * CHUNKS,
        in_specs=[vmem_spec()] * 5,
        out_specs=[vmem_spec()] * (1 + CHUNKS),
        compiler_params=pltpu.CompilerParams(vmem_limit_bytes=16 * MIB),
        cost_estimate=pl.CostEstimate(
            flops=600 * 10**6, bytes_accessed=5 * 10**6, transcendentals=0
        ),
        name="dispatch",
    )(heads, w_out, tokens, gain.reshape(1, width), pick)


def expert_kernel(rows_ref, up_ref, down_ref, out_ref):
    count, width = rows_ref.shape
    hidden = down_ref.shape[0]
    step = min(256, count)
    wide = 256

    def block(i, _):
        here = pl.ds(pl.multiple_of(i * step, step), step)
        rows = rows_ref[here, :]
        total = jnp.zeros((step, width), F32)
        for first in range(0, hidden, wide):
            last = min(first + wide, hidden)
            gate = jnp.dot(rows, up_ref[:, first:last], preferred_element_type=F32)
            value = jnp.dot(
                rows, up_ref[:, hidden + first : hidden + last], preferred_element_type=F32
            )
            active = (gate / (1.0 + jnp.exp(-gate)) * value).astype(BF16)
            total = total + jnp.dot(active, down_ref[first:last], preferred_element_type=F32)
        out_ref[here, :] = total.astype(BF16)
        return 0

    lax.fori_loop(0, count // step, block, 0)


def run_expert(rows, w_gateup, w_down):
    count, width = rows.shape
    hidden = w_down.shape[0]
    return pl.pallas_call(
        expert_kernel,
        out_shape=jax.ShapeDtypeStruct((count, width), BF16),
        in_specs=[vmem_spec()] * 3,
        out_specs=vmem_spec(),
        compiler_params=pltpu.CompilerParams(vmem_limit_bytes=24 * MIB),
        cost_estimate=pl.CostEstimate(
            flops=6 * count * width * hidden, bytes_accessed=9 * 10**6, transcendentals=count * hidden
        ),
        name="experts",
    )(rows, w_gateup, w_down)


def combine_kernel(mixed_ref, high_ref, low_ref, *refs):
    back, out_ref = refs[:-1], refs[-1]
    total = mixed_ref[...]
    start = 0
    for ref in back:
        count = ref.shape[0]
        rows = ref[...]
        total = total + jnp.dot(
            high_ref[:, start : start + count], rows, preferred_element_type=F32
        )
        total = total + jnp.dot(
            low_ref[:, start : start + count], rows, preferred_element_type=F32
        )
        start += count
    out_ref[...] = total.astype(BF16)


def combine(mixed, high, low, back):
    return pl.pallas_call(
        combine_kernel,
        out_shape=jax.ShapeDtypeStruct(mixed.shape, BF16),
        in_specs=[vmem_spec()] * (3 + len(back)),
        out_specs=vmem_spec(),
        compiler_params=pltpu.CompilerParams(vmem_limit_bytes=16 * MIB),
        cost_estimate=pl.CostEstimate(
            flops=540 * 10**6, bytes_accessed=4 * 10**6, transcendentals=0
        ),
        name="combine",
    )(mixed, high, low, *back)


def ring_gather(block, axis):
    size = lax.axis_size(axis)
    up = [(i, (i + 1) % size) for i in range(size)]
    down = [(i, (i - 1) % size) for i in range(size)]
    blocks, steps = [block], [0]
    forth = back = block
    for step in range(1, size // 2):
        forth = lax.ppermute(forth, axis, up)
        back = lax.ppermute(back, axis, down)
        blocks += [forth, back]
        steps += [-step, step]
    half = block.shape[0] // 2
    blocks += [lax.ppermute(forth[:half], axis, up), lax.ppermute(back[half:], axis, down)]
    steps += [size // 2]
    return blocks, steps


def per_device(
    tokens,
    chain_ids,
    route_ids,
    route_weights,
    attn_gain,
    ffn_gain,
    chain_bias,
    w_qkv,
    w_out,
    w_gateup,
    w_down,
):
    inputs = tokens[0]
    tok, width = inputs.shape
    ring = lax.axis_size("ctx")
    experts = lax.axis_size("expert")
    me = lax.axis_index("ctx").astype(jnp.int32).reshape(1)
    normed = rms_scale(inputs, attn_gain).astype(BF16)
    blocks, steps = ring_gather(normed, "ctx")

    small = jnp.concatenate([w_out.T, chain_ids.astype(BF16), jnp.zeros((7, tok), BF16)], axis=0)
    small = lax.all_gather(small, "ctx", axis=0)
    columns = w_out.shape[1]
    chains = small[:, columns : columns + 1].astype(F32)
    w_rows = small[:, :columns].transpose(1, 0, 2).reshape(columns, width)
    w_all = lax.all_gather(w_rows, "expert", axis=0, tiled=True)

    w_head = lax.all_to_all(
        jnp.broadcast_to(w_qkv[None], (experts,) + w_qkv.shape), "expert", 0, 0, tiled=True
    )
    pick, high, low = route_tables(route_ids[0], route_weights[0], experts, CAP)
    attended = attention(me, chain_bias, chains, w_head, blocks, steps)
    heads = lax.all_to_all(attended, "ctx", split_axis=0, concat_axis=0, tiled=True)
    mixed, *outgoing = dispatch(heads, w_all, inputs, ffn_gain, pick, experts, CAP)
    back = []
    for rows in outgoing:
        arrived = lax.all_to_all(rows, "expert", split_axis=0, concat_axis=0, tiled=True)
        result = run_expert(arrived.reshape(-1, width), w_gateup[0], w_down[0])
        back.append(
            lax.all_to_all(
                result.reshape(arrived.shape), "expert", split_axis=0, concat_axis=0, tiled=True
            ).reshape(-1, width)
        )
    return combine(mixed, high, low, back)[None]


def solution(mesh):
    placed = (
        P("expert", "ctx", None),
        P("expert", "ctx"),
        P("expert", "ctx", None),
        P("expert", "ctx", None),
        P(),
        P(),
        P(),
        P(None, "expert", "ctx"),
        P("ctx", "expert"),
        P("expert", None, None),
        P("expert", None, None),
    )
    return jax.shard_map(
        per_device, mesh=mesh, in_specs=placed, out_specs=P("expert", "ctx", None), check_vma=False
    )
```

```python
import functools
import math

import jax
import jax.numpy as jnp
from jax import lax
from jax.experimental import pallas as pl
from jax.experimental.pallas import tpu as pltpu
from jax.sharding import PartitionSpec as P

F32 = jnp.float32
BF16 = jnp.bfloat16
MIB = 1 << 20
CAP = 32
EXTRA = 16
WIDE = 256


def vmem_spec():
    return pl.BlockSpec(memory_space=pltpu.VMEM)


def smem_spec():
    return pl.BlockSpec(memory_space=pltpu.SMEM)


def rms_scale(values, gain):
    wide = values.astype(F32)
    return wide * lax.rsqrt(jnp.mean(wide * wide, axis=-1, keepdims=True) + 1e-05) * gain


def slot_parts(shape, dim, cap):
    slot = lax.broadcasted_iota(jnp.int32, shape, dim)
    return slot // cap, lax.rem(slot, cap)


def pick_kernel(cap, ids_ref, pick_ref):
    topk, tok = ids_ref.shape
    slots = pick_ref.shape[0]
    experts = slots // cap
    named = jnp.zeros((experts, tok), F32)
    sub = lax.broadcasted_iota(jnp.int32, (experts, tok), 0)
    for route in range(topk):
        named = named + jnp.where(ids_ref[route : route + 1, :] == sub, 1.0, 0.0)
    row = lax.broadcasted_iota(jnp.int32, (tok, tok), 0)
    col = lax.broadcasted_iota(jnp.int32, (tok, tok), 1)
    before = jnp.where(row < col, 1.0, 0.0).astype(BF16)
    rank = jnp.dot(named.astype(BF16), before, preferred_element_type=F32)
    mine = jnp.where(named > 0.5, rank, -1.0).astype(BF16)
    expert_of, place_of = slot_parts((slots, experts), 0, cap)
    spread = jnp.where(
        lax.broadcasted_iota(jnp.int32, (slots, experts), 1) == expert_of, 1.0, 0.0
    ).astype(BF16)
    here = jnp.dot(spread, mine, preferred_element_type=F32) == place_of[:, 0:1].astype(F32)
    pick_ref[...] = jnp.where(here, 1.0, 0.0).astype(BF16)


def pick_table(ids, experts, cap):
    tok = ids.shape[0]
    return pl.pallas_call(
        functools.partial(pick_kernel, cap),
        out_shape=jax.ShapeDtypeStruct((experts * cap, tok), BF16),
        in_specs=[vmem_spec()],
        out_specs=vmem_spec(),
        compiler_params=pltpu.CompilerParams(vmem_limit_bytes=8 * MIB),
        cost_estimate=pl.CostEstimate(flops=10**8, bytes_accessed=10**6, transcendentals=0),
        name="pick_table",
    )(ids.T)


def gate_kernel(cap, ids_ref, weights_ref, high_ref, low_ref):
    tok, topk = ids_ref.shape
    slots = high_ref.shape[1]
    experts = slots // cap
    named = jnp.zeros((tok, experts), F32)
    gates = jnp.zeros((tok, experts), F32)
    lane = lax.broadcasted_iota(jnp.int32, (tok, experts), 1)
    for route in range(topk):
        hit = ids_ref[:, route : route + 1] == lane
        named = named + jnp.where(hit, 1.0, 0.0)
        gates = gates + jnp.where(hit, weights_ref[:, route : route + 1], 0.0)
    row = lax.broadcasted_iota(jnp.int32, (tok, tok), 0)
    col = lax.broadcasted_iota(jnp.int32, (tok, tok), 1)
    before = jnp.where(col < row, 1.0, 0.0).astype(BF16)
    rank = jnp.dot(before, named.astype(BF16), preferred_element_type=F32)
    expert_of, place_of = slot_parts((experts, slots), 1, cap)
    spread = jnp.where(
        lax.broadcasted_iota(jnp.int32, (experts, slots), 0) == expert_of, 1.0, 0.0
    ).astype(BF16)
    mine = jnp.where(named > 0.5, rank, -1.0).astype(BF16)
    here = jnp.dot(mine, spread, preferred_element_type=F32) == place_of[0:1, :].astype(F32)
    high = gates.astype(BF16)
    low = (gates - high.astype(F32)).astype(BF16)
    for part, ref in ((high, high_ref), (low, low_ref)):
        wide = jnp.dot(part, spread, preferred_element_type=F32)
        ref[...] = jnp.where(here, wide, 0.0).astype(BF16)


def gate_tables(ids, weights, experts, cap):
    tok = ids.shape[0]
    return pl.pallas_call(
        functools.partial(gate_kernel, cap),
        out_shape=[jax.ShapeDtypeStruct((tok, experts * cap), BF16)] * 2,
        in_specs=[vmem_spec()] * 2,
        out_specs=[vmem_spec()] * 2,
        compiler_params=pltpu.CompilerParams(vmem_limit_bytes=8 * MIB),
        cost_estimate=pl.CostEstimate(flops=10**8, bytes_accessed=10**6, transcendentals=0),
        name="gate_tables",
    )(ids, weights)


def attention_kernel(
    steps, me_ref, bias_ref, chain_ref, w_ref, *refs
):
    blocks, (out_ref, w_buf, q_buf, k_buf, v_buf) = refs[:-5], refs[-5:]
    me = me_ref[0]
    ring = len(steps)
    tok = out_ref.shape[1]
    head_dim = out_ref.shape[2]
    width = w_buf.shape[0]
    part = width // w_ref.shape[0]
    for i in range(3):
        w_buf[:, i * head_dim : (i + 1) * head_dim] = w_ref[:, i * part : (i + 1) * part].reshape(
            width, head_dim
        )
    start = 0
    for block in blocks:
        rows = block.shape[0]
        both = jnp.dot(block[...], w_buf[...], preferred_element_type=F32).astype(BF16)
        q_buf[start : start + rows] = both[:, :head_dim]
        k_buf[start : start + rows] = both[:, head_dim : 2 * head_dim]
        v_buf[start : start + rows] = both[:, 2 * head_dim :]
        start += rows
    owner = [lax.rem(me + (s + ring), ring) for s in steps]
    rows_of = [chain_ref[o] for o in owner]
    key_chain = jnp.concatenate(rows_of, axis=1)
    scale = 1.0 / math.sqrt(head_dim)
    bias = bias_ref[me]
    pair = 2
    for first in range(0, ring, pair):
        query_chain = jnp.concatenate(
            [
                jnp.broadcast_to(rows_of[first + j], (tok, tok)).T
                for j in range(pair)
            ],
            axis=0,
        )
        query_chain = jnp.concatenate([query_chain] * ring, axis=1)
        query = q_buf[first * tok : (first + pair) * tok]
        scores = (
            lax.dot_general(
                query, k_buf[...], (((1,), (1,)), ((), ())), preferred_element_type=F32
            )
            * scale
        )
        scores = scores + jnp.where(query_chain == key_chain, bias, 0.0)
        top = jnp.max(scores, axis=-1, keepdims=True)
        raised = jnp.exp(scores - top)
        probs = (raised * (1.0 / jnp.sum(raised, axis=-1, keepdims=True))).astype(BF16)
        mixed = jnp.dot(probs, v_buf[...], preferred_element_type=F32).astype(BF16)
        for j in range(pair):
            out_ref[owner[first + j]] = mixed[j * tok : (j + 1) * tok]


def attention(me, bias, chains, weights, blocks, steps):
    ring = len(steps)
    tok = chains.shape[2]
    head_dim = weights.shape[2]
    width = blocks[0].shape[1]
    length = ring * tok
    return pl.pallas_call(
        functools.partial(attention_kernel, steps),
        out_shape=jax.ShapeDtypeStruct((ring, tok, head_dim), BF16),
        in_specs=[smem_spec(), smem_spec()] + [vmem_spec()] * (2 + len(blocks)),
        out_specs=vmem_spec(),
        scratch_shapes=[
            pltpu.VMEM((width, 3 * head_dim), BF16),
            pltpu.VMEM((length, head_dim), BF16),
            pltpu.VMEM((length, head_dim), BF16),
            pltpu.VMEM((length, head_dim), BF16),
        ],
        compiler_params=pltpu.CompilerParams(vmem_limit_bytes=16 * MIB),
        cost_estimate=pl.CostEstimate(
            flops=1400 * 10**6, bytes_accessed=3 * 10**6, transcendentals=10**6
        ),
        name="attention",
    )(me, bias, chains, weights, *blocks)


def dispatch_kernel(
    core_ref, heads_ref, own_ref, other_ref, tokens_ref, gain_ref, pick_ref, mixed_ref, out_ref
):
    core = core_ref[0]
    half = heads_ref.shape[0] // 2
    width = tokens_ref.shape[1]
    mixed = tokens_ref[...].astype(F32)
    columns = own_ref.shape[1] // half
    for ref, side in ((own_ref, core), (other_ref, 1 - core)):
        local = jnp.concatenate([heads_ref[side * half + j] for j in range(half)], axis=1)
        w_out = jnp.concatenate(
            [
                ref[:, j * columns : (j + 1) * columns].reshape(width, heads_ref.shape[2])
                for j in range(half)
            ],
            axis=1,
        )
        mixed = mixed + lax.dot_general(
            local, w_out, (((1,), (1,)), ((), ())), preferred_element_type=F32
        )
    mixed_ref[...] = mixed
    ffn_in = (
        mixed * lax.rsqrt(jnp.mean(mixed * mixed, axis=-1, keepdims=True) + 1e-05) * gain_ref[...]
    ).astype(BF16)
    out_ref[...] = (
        jnp.dot(pick_ref[...], ffn_in, preferred_element_type=F32)
        .astype(BF16)
        .reshape(out_ref.shape)
    )


def dispatch(core, heads, own, other, tokens, gain, pick, experts, cap):
    tok, width = tokens.shape
    return pl.pallas_call(
        dispatch_kernel,
        out_shape=[
            jax.ShapeDtypeStruct((tok, width), F32),
            jax.ShapeDtypeStruct((experts, cap, width), BF16),
        ],
        in_specs=[smem_spec()] + [vmem_spec()] * 6,
        out_specs=[vmem_spec()] * 2,
        compiler_params=pltpu.CompilerParams(vmem_limit_bytes=16 * MIB),
        cost_estimate=pl.CostEstimate(
            flops=600 * 10**6, bytes_accessed=5 * 10**6, transcendentals=0
        ),
        name="dispatch",
    )(core, heads, own, other, tokens, gain.reshape(1, width), pick)


def expert_kernel(rows_ref, up_ref, down_ref, out_ref):
    hidden = down_ref.shape[0]
    rows = rows_ref[...]
    total = jnp.zeros(rows.shape, F32)
    for first in range(0, hidden, WIDE):
        last = min(first + WIDE, hidden)
        gate = jnp.dot(rows, up_ref[:, first:last], preferred_element_type=F32)
        value = jnp.dot(
            rows, up_ref[:, hidden + first : hidden + last], preferred_element_type=F32
        )
        active = (gate / (1.0 + jnp.exp(-gate)) * value).astype(BF16)
        total = total + jnp.dot(active, down_ref[first:last], preferred_element_type=F32)
    out_ref[...] = total.astype(BF16)


def run_expert(rows, w_gateup, w_down):
    count, width = rows.shape
    hidden = w_down.shape[0]
    return pl.pallas_call(
        expert_kernel,
        out_shape=jax.ShapeDtypeStruct((count, width), BF16),
        in_specs=[vmem_spec()] * 3,
        out_specs=vmem_spec(),
        compiler_params=pltpu.CompilerParams(vmem_limit_bytes=24 * MIB),
        cost_estimate=pl.CostEstimate(
            flops=6 * count * width * hidden, bytes_accessed=9 * 10**6, transcendentals=count * hidden
        ),
        name="experts",
    )(rows, w_gateup, w_down)


def combine_kernel(mixed_ref, high_ref, low_ref, back_ref, out_ref):
    rows = back_ref[...]
    total = mixed_ref[...] + jnp.dot(high_ref[...], rows, preferred_element_type=F32)
    total = total + jnp.dot(low_ref[...], rows, preferred_element_type=F32)
    out_ref[...] = total.astype(BF16)


def combine(mixed, high, low, back):
    return pl.pallas_call(
        combine_kernel,
        out_shape=jax.ShapeDtypeStruct(mixed.shape, BF16),
        in_specs=[vmem_spec()] * 4,
        out_specs=vmem_spec(),
        compiler_params=pltpu.CompilerParams(vmem_limit_bytes=16 * MIB),
        cost_estimate=pl.CostEstimate(
            flops=540 * 10**6, bytes_accessed=4 * 10**6, transcendentals=0
        ),
        name="combine",
    )(mixed, high, low, back)


def ring_gather(block, axis):
    size = lax.axis_size(axis)
    up = [(i, (i + 1) % size) for i in range(size)]
    down = [(i, (i - 1) % size) for i in range(size)]
    blocks, steps = [block], [0]
    forth = back = block
    for step in range(1, size // 2):
        forth = lax.ppermute(forth, axis, up)
        back = lax.ppermute(back, axis, down)
        blocks += [forth, back]
        steps += [-step, step]
    half = block.shape[0] // 2
    blocks += [lax.ppermute(forth[:half], axis, up), lax.ppermute(back[half:], axis, down)]
    steps += [size // 2]
    return blocks, steps


def per_device(
    tokens,
    chain_ids,
    route_ids,
    route_weights,
    attn_gain,
    ffn_gain,
    chain_bias,
    w_qkv,
    w_out,
    w_gateup,
    w_down,
):
    inputs = tokens[0]
    tok, width = inputs.shape
    ring = lax.axis_size("ctx")
    experts = lax.axis_size("expert")
    me = lax.axis_index("ctx").astype(jnp.int32).reshape(1)
    core = lax.rem(lax.axis_index("expert").astype(jnp.int32), 2).reshape(1)
    columns = w_out.shape[1]
    head_dim = tok

    normed = rms_scale(inputs, attn_gain).astype(BF16)
    small = jnp.concatenate(
        [w_out.T, chain_ids.astype(BF16), jnp.zeros((EXTRA - 1, tok), BF16)], axis=0
    )
    small, normed = lax.optimization_barrier((small, normed))
    small = lax.all_to_all(
        jnp.broadcast_to(small[None], (ring,) + small.shape), "ctx", 0, 0, tiled=True
    )
    chains = small[:, columns : columns + 1].astype(F32)

    blocks, steps = ring_gather(normed, "ctx")

    w_rows = small[:, :columns].reshape(2, -1, head_dim)
    mine = w_qkv.reshape(1, -1, head_dim)
    mine, blocks[1], blocks[2] = lax.optimization_barrier((mine, blocks[1], blocks[2]))
    both = jnp.concatenate([jnp.broadcast_to(mine, (2,) + mine.shape[1:]), w_rows], axis=1)
    plane = lax.all_to_all(
        jnp.broadcast_to(both[None], (experts // 2,) + both.shape).reshape(
            (experts,) + both.shape[1:]
        ),
        "expert",
        0,
        0,
        tiled=True,
    )
    plane, blocks[-2], blocks[-1] = lax.optimization_barrier((plane, blocks[-2], blocks[-1]))
    w_head = plane[:, : mine.shape[1]]

    pick = pick_table(route_ids[0], experts, CAP)
    high, low = gate_tables(route_ids[0], route_weights[0], experts, CAP)
    attended = attention(me, chain_bias, chains, w_head, blocks, steps)
    plane, attended = lax.optimization_barrier((plane, attended))
    own = plane[:, mine.shape[1] :]
    other = lax.ppermute(own, "expert", [(i, i ^ 1) for i in range(experts)])
    heads = lax.all_to_all(attended, "ctx", split_axis=0, concat_axis=0, tiled=True)
    pick, high, low = lax.optimization_barrier((pick, high, low))
    mixed, outgoing = dispatch(core, heads, own, other, inputs, ffn_gain, pick, experts, CAP)
    arrived = lax.all_to_all(outgoing, "expert", split_axis=0, concat_axis=0, tiled=True)
    result = run_expert(arrived.reshape(-1, width), w_gateup[0], w_down[0])
    back = lax.all_to_all(
        result.reshape(arrived.shape), "expert", split_axis=0, concat_axis=0, tiled=True
    )
    return combine(mixed, high, low, back.reshape(-1, width))[None]


def solution(mesh):
    placed = (
        P("expert", "ctx", None),
        P("expert", "ctx"),
        P("expert", "ctx", None),
        P("expert", "ctx", None),
        P(),
        P(),
        P(),
        P(None, "expert", "ctx"),
        P("ctx", "expert"),
        P("expert", None, None),
        P("expert", None, None),
    )
    return jax.shard_map(
        per_device, mesh=mesh, in_specs=placed, out_specs=P("expert", "ctx", None), check_vma=False
    )
```

```python
import functools
import math

import jax
import jax.numpy as jnp
from jax import lax
from jax.experimental import pallas as pl
from jax.experimental.pallas import tpu as pltpu
from jax.sharding import PartitionSpec as P

F32 = jnp.float32
BF16 = jnp.bfloat16
MIB = 1 << 20
CAP = 32
EXTRA = 16
CHAINS = 8
WIDE = 256


def vmem_spec():
    return pl.BlockSpec(memory_space=pltpu.VMEM)


def smem_spec():
    return pl.BlockSpec(memory_space=pltpu.SMEM)


def start_kernel(tokens_ref, gain_ref, w_ref, chain_ref, normed_ref, small_ref):
    wide = tokens_ref[...].astype(F32)
    normed_ref[...] = (
        wide * lax.rsqrt(jnp.mean(wide * wide, axis=-1, keepdims=True) + 1e-05) * gain_ref[...]
    ).astype(BF16)
    columns = w_ref.shape[0]
    chains = jnp.broadcast_to(chain_ref[...].astype(F32), (EXTRA, w_ref.shape[1])).astype(BF16)
    for i in range(small_ref.shape[0]):
        small_ref[i, :columns] = w_ref[...]
        small_ref[i, columns:] = chains


def start(tokens, gain, w_out, chain_ids, ring):
    tok, width = tokens.shape
    columns = w_out.shape[1]
    return pl.pallas_call(
        start_kernel,
        out_shape=[
            jax.ShapeDtypeStruct((tok, width), BF16),
            jax.ShapeDtypeStruct((ring, columns + EXTRA, tok), BF16),
        ],
        in_specs=[vmem_spec()] * 4,
        out_specs=[vmem_spec()] * 2,
        compiler_params=pltpu.CompilerParams(vmem_limit_bytes=60 * MIB),
        cost_estimate=pl.CostEstimate(flops=10**6, bytes_accessed=10**6, transcendentals=0),
        name="start",
    )(tokens, gain.reshape(1, width), w_out.T, chain_ids)


def plane_kernel(small_ref, w_ref, plane_ref, chain_ref, parts, left):
    ring, rows, _ = small_ref.shape
    columns = rows - EXTRA
    own, half = w_ref.shape[0], ring // 2
    chain_ref[...] = small_ref[:, columns:].astype(F32)[:, 0:1]
    copies = []
    for core in range(2):
        parts[core, :own] = w_ref[...]
        for j in range(half):
            first = own + j * columns
            parts[core, first : first + columns] = small_ref[core * half + j, :columns]
        for i in range(core, plane_ref.shape[0], 2):
            copies.append(pltpu.make_async_copy(parts.at[core], plane_ref.at[i], left.at[i]))
            copies[-1].start()
    for copy in copies:
        copy.wait()


def plane_parts(small, w_head, experts):
    ring, rows, lanes = small.shape
    count = w_head.shape[0] + ring // 2 * (rows - EXTRA)
    return pl.pallas_call(
        plane_kernel,
        out_shape=[
            jax.ShapeDtypeStruct((experts, count, lanes), BF16),
            jax.ShapeDtypeStruct((ring, 1, lanes), F32),
        ],
        in_specs=[vmem_spec()] * 2,
        out_specs=[pl.BlockSpec(memory_space=pltpu.HBM), vmem_spec()],
        scratch_shapes=[pltpu.VMEM((2, count, lanes), BF16), pltpu.SemaphoreType.DMA((experts,))],
        compiler_params=pltpu.CompilerParams(vmem_limit_bytes=60 * MIB),
        cost_estimate=pl.CostEstimate(flops=10**6, bytes_accessed=2 * 10**6, transcendentals=0),
        name="plane_parts",
    )(small, w_head)


def slot_parts(shape, dim, cap):
    slot = lax.broadcasted_iota(jnp.int32, shape, dim)
    return slot // cap, lax.rem(slot, cap)


def pick_kernel(cap, ids_ref, pick_ref):
    topk, tok = ids_ref.shape
    slots = pick_ref.shape[0]
    experts = slots // cap
    named = jnp.zeros((experts, tok), F32)
    sub = lax.broadcasted_iota(jnp.int32, (experts, tok), 0)
    for route in range(topk):
        named = named + jnp.where(ids_ref[route : route + 1, :] == sub, 1.0, 0.0)
    row = lax.broadcasted_iota(jnp.int32, (tok, tok), 0)
    col = lax.broadcasted_iota(jnp.int32, (tok, tok), 1)
    before = jnp.where(row < col, 1.0, 0.0).astype(BF16)
    rank = jnp.dot(named.astype(BF16), before, preferred_element_type=F32)
    mine = jnp.where(named > 0.5, rank, -1.0).astype(BF16)
    expert_of, place_of = slot_parts((slots, experts), 0, cap)
    spread = jnp.where(
        lax.broadcasted_iota(jnp.int32, (slots, experts), 1) == expert_of, 1.0, 0.0
    ).astype(BF16)
    here = jnp.dot(spread, mine, preferred_element_type=F32) == place_of[:, 0:1].astype(F32)
    pick_ref[...] = jnp.where(here, 1.0, 0.0).astype(BF16)


def pick_table(ids, experts, cap):
    tok = ids.shape[0]
    return pl.pallas_call(
        functools.partial(pick_kernel, cap),
        out_shape=jax.ShapeDtypeStruct((experts * cap, tok), BF16),
        in_specs=[vmem_spec()],
        out_specs=vmem_spec(),
        compiler_params=pltpu.CompilerParams(vmem_limit_bytes=8 * MIB),
        cost_estimate=pl.CostEstimate(flops=10**8, bytes_accessed=10**6, transcendentals=0),
        name="pick_table",
    )(ids.T)


def gate_kernel(cap, ids_ref, weights_ref, gate_ref):
    tok, topk = ids_ref.shape
    slots = gate_ref.shape[1]
    experts = slots // cap
    named = jnp.zeros((tok, experts), F32)
    gates = jnp.zeros((tok, experts), F32)
    lane = lax.broadcasted_iota(jnp.int32, (tok, experts), 1)
    for route in range(topk):
        hit = ids_ref[:, route : route + 1] == lane
        named = named + jnp.where(hit, 1.0, 0.0)
        gates = gates + jnp.where(hit, weights_ref[:, route : route + 1], 0.0)
    row = lax.broadcasted_iota(jnp.int32, (tok, tok), 0)
    col = lax.broadcasted_iota(jnp.int32, (tok, tok), 1)
    before = jnp.where(col < row, 1.0, 0.0).astype(BF16)
    rank = jnp.dot(before, named.astype(BF16), preferred_element_type=F32)
    expert_of, place_of = slot_parts((experts, slots), 1, cap)
    spread = jnp.where(
        lax.broadcasted_iota(jnp.int32, (experts, slots), 0) == expert_of, 1.0, 0.0
    ).astype(BF16)
    mine = jnp.where(named > 0.5, rank, -1.0).astype(BF16)
    here = jnp.dot(mine, spread, preferred_element_type=F32) == place_of[0:1, :].astype(F32)
    high = gates.astype(BF16)
    low = (gates - high.astype(F32)).astype(BF16)
    for i, part in enumerate((high, low)):
        wide = jnp.dot(part, spread, preferred_element_type=F32)
        gate_ref[i * tok : (i + 1) * tok] = jnp.where(here, wide, 0.0).astype(BF16)


def gate_tables(ids, weights, experts, cap):
    tok = ids.shape[0]
    return pl.pallas_call(
        functools.partial(gate_kernel, cap),
        out_shape=jax.ShapeDtypeStruct((2 * tok, experts * cap), BF16),
        in_specs=[vmem_spec()] * 2,
        out_specs=vmem_spec(),
        compiler_params=pltpu.CompilerParams(vmem_limit_bytes=8 * MIB),
        cost_estimate=pl.CostEstimate(flops=10**8, bytes_accessed=10**6, transcendentals=0),
        name="gate_tables",
    )(ids, weights)


def attention_kernel(steps, me_ref, bias_ref, chain_ref, w_ref, *refs):
    blocks, (out_ref, w_buf, q_buf, k_buf, v_buf) = refs[:-5], refs[-5:]
    me = me_ref[0]
    ring = len(steps)
    tok = out_ref.shape[1]
    head_dim = out_ref.shape[2]
    width = w_buf.shape[0]
    part = width // w_ref.shape[0]
    for i in range(3):
        w_buf[:, i * head_dim : (i + 1) * head_dim] = w_ref[:, i * part : (i + 1) * part].reshape(
            width, head_dim
        )
    start = 0
    for block in blocks:
        here = slice(start, start + block.shape[0])
        both = jnp.dot(block[...], w_buf[...], preferred_element_type=F32).astype(BF16)
        q_buf[here, :head_dim] = both[:, :head_dim]
        k_buf[here, :head_dim] = both[:, head_dim : 2 * head_dim]
        v_buf[here] = both[:, 2 * head_dim :]
        start += block.shape[0]
    scale = 1.0 / math.sqrt(head_dim)
    lane = lax.broadcasted_iota(jnp.int32, (tok, tok), 1)
    named = jnp.where(lane < 3 * CHAINS, lax.rem(lane, CHAINS), -1).astype(F32)
    whole = jnp.full((tok, tok), bias_ref[me] * math.sqrt(head_dim), F32)
    first = whole.astype(BF16).astype(F32)
    second = (whole - first).astype(BF16).astype(F32)
    third = whole - first - second
    bias = jnp.where(lane < CHAINS, first, jnp.where(lane < 2 * CHAINS, second, third))
    owner = [lax.rem(me + (s + ring), ring) for s in steps]
    for i in range(ring):
        same = jnp.broadcast_to(chain_ref[owner[i]], (tok, tok)).T == named
        here = slice(i * tok, (i + 1) * tok)
        k_buf[here, head_dim:] = jnp.where(same, 1.0, 0.0).astype(BF16)
        q_buf[here, head_dim:] = jnp.where(same, bias, 0.0).astype(BF16)
    count = 4
    for start in range(0, ring, count):
        scores = lax.dot_general(
            q_buf[start * tok : (start + count) * tok],
            k_buf[...],
            (((1,), (1,)), ((), ())),
            preferred_element_type=F32,
        )
        top = jnp.max(scores, axis=-1, keepdims=True)
        raised = jnp.exp2((scores - top) * (scale * math.log2(math.e)))
        probs = (raised * (1.0 / jnp.sum(raised, axis=-1, keepdims=True))).astype(BF16)
        mixed = jnp.dot(probs, v_buf[...], preferred_element_type=F32).astype(BF16)
        for j in range(count):
            out_ref[owner[start + j]] = mixed[j * tok : (j + 1) * tok]


def attention(me, bias, chains, weights, blocks, steps):
    ring = len(steps)
    tok = chains.shape[2]
    head_dim = weights.shape[2]
    width = blocks[0].shape[1]
    length = ring * tok
    return pl.pallas_call(
        functools.partial(attention_kernel, steps),
        out_shape=jax.ShapeDtypeStruct((ring, tok, head_dim), BF16),
        in_specs=[smem_spec(), smem_spec()] + [vmem_spec()] * (2 + len(blocks)),
        out_specs=vmem_spec(),
        scratch_shapes=[
            pltpu.VMEM((width, 3 * head_dim), BF16),
            pltpu.VMEM((length, head_dim + tok), BF16),
            pltpu.VMEM((length, head_dim + tok), BF16),
            pltpu.VMEM((length, head_dim), BF16),
        ],
        compiler_params=pltpu.CompilerParams(vmem_limit_bytes=16 * MIB),
        cost_estimate=pl.CostEstimate(
            flops=1400 * 10**6, bytes_accessed=3 * 10**6, transcendentals=10**6
        ),
        name="attention",
    )(me, bias, chains, weights, *blocks)


def dispatch_kernel(core_ref, heads_ref, *refs):
    parts, (tokens_ref, gain_ref, pick_ref, mixed_ref, out_ref) = refs[:-5], refs[-5:]
    core = core_ref[0]
    half = heads_ref.shape[0] // 2
    width = tokens_ref.shape[1]
    mixed = tokens_ref[...].astype(F32)
    for own, side in ((0, core), (half, 1 - core)):
        local = jnp.concatenate([heads_ref[side * half + j] for j in range(half)], axis=1)
        w_out = jnp.concatenate(
            [parts[own + j][...].reshape(width, heads_ref.shape[2]) for j in range(half)], axis=1
        )
        mixed = mixed + lax.dot_general(
            local, w_out, (((1,), (1,)), ((), ())), preferred_element_type=F32
        )
    mixed_ref[...] = mixed
    ffn_in = (
        mixed * lax.rsqrt(jnp.mean(mixed * mixed, axis=-1, keepdims=True) + 1e-05) * gain_ref[...]
    ).astype(BF16)
    out_ref[...] = (
        jnp.dot(pick_ref[...], ffn_in, preferred_element_type=F32)
        .astype(BF16)
        .reshape(out_ref.shape)
    )


def dispatch(core, heads, parts, tokens, gain, pick, experts, cap):
    tok, width = tokens.shape
    return pl.pallas_call(
        dispatch_kernel,
        out_shape=[
            jax.ShapeDtypeStruct((tok, width), F32),
            jax.ShapeDtypeStruct((experts, cap, width), BF16),
        ],
        in_specs=[smem_spec()] + [vmem_spec()] * (4 + len(parts)),
        out_specs=[vmem_spec()] * 2,
        compiler_params=pltpu.CompilerParams(vmem_limit_bytes=16 * MIB),
        cost_estimate=pl.CostEstimate(
            flops=600 * 10**6, bytes_accessed=5 * 10**6, transcendentals=0
        ),
        name="dispatch",
    )(core, heads, *parts, tokens, gain.reshape(1, width), pick)


def expert_kernel(rows_ref, up_ref, down_ref, out_ref):
    hidden = down_ref.shape[0]
    rows = rows_ref[...]
    total = jnp.zeros(rows.shape, F32)
    for first in range(0, hidden, WIDE):
        last = min(first + WIDE, hidden)
        gate = jnp.dot(rows, up_ref[:, first:last], preferred_element_type=F32)
        value = jnp.dot(
            rows, up_ref[:, hidden + first : hidden + last], preferred_element_type=F32
        )
        active = (gate / (1.0 + jnp.exp(-gate)) * value).astype(BF16)
        total = total + jnp.dot(active, down_ref[first:last], preferred_element_type=F32)
    out_ref[...] = total.astype(BF16)


def run_expert(rows, w_gateup, w_down):
    count, width = rows.shape
    hidden = w_down.shape[0]
    return pl.pallas_call(
        expert_kernel,
        out_shape=jax.ShapeDtypeStruct((count, width), BF16),
        in_specs=[vmem_spec()] * 3,
        out_specs=vmem_spec(),
        compiler_params=pltpu.CompilerParams(vmem_limit_bytes=24 * MIB),
        cost_estimate=pl.CostEstimate(
            flops=6 * count * width * hidden, bytes_accessed=9 * 10**6, transcendentals=count * hidden
        ),
        name="experts",
    )(rows, w_gateup, w_down)


def combine_kernel(mixed_ref, gate_ref, back_ref, out_ref):
    tok = mixed_ref.shape[0]
    both = jnp.dot(gate_ref[...], back_ref[...], preferred_element_type=F32)
    out_ref[...] = (mixed_ref[...] + (both[:tok] + both[tok:])).astype(BF16)


def combine(mixed, gates, back):
    return pl.pallas_call(
        combine_kernel,
        out_shape=jax.ShapeDtypeStruct(mixed.shape, BF16),
        in_specs=[vmem_spec()] * 3,
        out_specs=vmem_spec(),
        compiler_params=pltpu.CompilerParams(vmem_limit_bytes=16 * MIB),
        cost_estimate=pl.CostEstimate(
            flops=540 * 10**6, bytes_accessed=4 * 10**6, transcendentals=0
        ),
        name="combine",
    )(mixed, gates, back)


def ring_gather(block, axis):
    size = lax.axis_size(axis)
    up = [(i, (i + 1) % size) for i in range(size)]
    down = [(i, (i - 1) % size) for i in range(size)]
    blocks, steps = [block], [0]
    forth = back = block
    for step in range(1, size // 2):
        forth = lax.ppermute(forth, axis, up)
        back = lax.ppermute(back, axis, down)
        blocks += [forth, back]
        steps += [-step, step]
    half = block.shape[0] // 2
    blocks += [lax.ppermute(forth[:half], axis, up), lax.ppermute(back[half:], axis, down)]
    steps += [size // 2]
    return blocks, steps


def per_device(
    tokens,
    chain_ids,
    route_ids,
    route_weights,
    attn_gain,
    ffn_gain,
    chain_bias,
    w_qkv,
    w_out,
    w_gateup,
    w_down,
):
    inputs = tokens[0]
    tok, width = inputs.shape
    ring = lax.axis_size("ctx")
    experts = lax.axis_size("expert")
    me = lax.axis_index("ctx").astype(jnp.int32).reshape(1)
    core = lax.rem(lax.axis_index("expert").astype(jnp.int32), 2).reshape(1)
    normed, small = start(inputs, attn_gain, w_out, chain_ids, ring)
    blocks, steps = ring_gather(normed, "ctx")

    small = lax.all_to_all(small, "ctx", 0, 0, tiled=True)
    w_head = w_qkv.reshape(-1, w_qkv.shape[2])
    w_head, blocks[1], blocks[2] = lax.optimization_barrier((w_head, blocks[1], blocks[2]))
    parts, chains = plane_parts(small, w_head, experts)
    plane = lax.all_to_all(parts, "expert", 0, 0, tiled=True)
    plane, blocks[-2], blocks[-1] = lax.optimization_barrier((plane, blocks[-2], blocks[-1]))

    mine = w_head.shape[0]
    attended = attention(me, chain_bias, chains, plane[:, :mine], blocks, steps)
    plane, attended = lax.optimization_barrier((plane, attended))
    swap = [(i, i ^ 1) for i in range(experts)]
    rest = plane.shape[1] - mine
    own = [plane[:, mine + i * rest // 4 : mine + (i + 1) * rest // 4] for i in range(4)]
    other = [lax.ppermute(part, "expert", swap) for part in own]
    heads = lax.all_to_all(attended, "ctx", split_axis=0, concat_axis=0, tiled=True)
    pick = pick_table(route_ids[0], experts, CAP)
    gates = gate_tables(route_ids[0], route_weights[0], experts, CAP)
    pick, gates = lax.optimization_barrier((pick, gates))
    mixed, outgoing = dispatch(core, heads, own + other, inputs, ffn_gain, pick, experts, CAP)
    arrived = lax.all_to_all(outgoing, "expert", split_axis=0, concat_axis=0, tiled=True)
    result = run_expert(arrived.reshape(-1, width), w_gateup[0], w_down[0])
    back = lax.all_to_all(
        result.reshape(arrived.shape), "expert", split_axis=0, concat_axis=0, tiled=True
    )
    return combine(mixed, gates, back.reshape(-1, width))[None]


def solution(mesh):
    placed = (
        P("expert", "ctx", None),
        P("expert", "ctx"),
        P("expert", "ctx", None),
        P("expert", "ctx", None),
        P(),
        P(),
        P(),
        P(None, "expert", "ctx"),
        P("ctx", "expert"),
        P("expert", None, None),
        P("expert", None, None),
    )
    return jax.shard_map(
        per_device, mesh=mesh, in_specs=placed, out_specs=P("expert", "ctx", None), check_vma=False
    )
```

```python
import functools
import math

import jax
import jax.numpy as jnp
from jax import lax
from jax.experimental import pallas as pl
from jax.experimental.pallas import tpu as pltpu
from jax.sharding import PartitionSpec as P

F32 = jnp.float32
BF16 = jnp.bfloat16
MIB = 1 << 20
CAP = 32
EXTRA = 16
CHAINS = 8
WIDE = 256


def vmem_spec():
    return pl.BlockSpec(memory_space=pltpu.VMEM)


def smem_spec():
    return pl.BlockSpec(memory_space=pltpu.SMEM)


def start_kernel(tokens_ref, gain_ref, w_ref, chain_ref, normed_ref, small_ref):
    wide = tokens_ref[...].astype(F32)
    normed_ref[...] = (
        wide * lax.rsqrt(jnp.mean(wide * wide, axis=-1, keepdims=True) + 1e-05) * gain_ref[...]
    ).astype(BF16)
    columns = w_ref.shape[0]
    chains = jnp.broadcast_to(chain_ref[...].astype(F32), (EXTRA, w_ref.shape[1])).astype(BF16)
    for i in range(small_ref.shape[0]):
        small_ref[i, :columns] = w_ref[...]
        small_ref[i, columns:] = chains


def start(tokens, gain, w_out, chain_ids, ring):
    tok, width = tokens.shape
    columns = w_out.shape[1]
    return pl.pallas_call(
        start_kernel,
        out_shape=[
            jax.ShapeDtypeStruct((tok, width), BF16),
            jax.ShapeDtypeStruct((ring, columns + EXTRA, tok), BF16),
        ],
        in_specs=[vmem_spec()] * 4,
        out_specs=[vmem_spec()] * 2,
        compiler_params=pltpu.CompilerParams(vmem_limit_bytes=60 * MIB),
        cost_estimate=pl.CostEstimate(flops=10**6, bytes_accessed=10**6, transcendentals=0),
        name="start",
    )(tokens, gain.reshape(1, width), w_out.T, chain_ids)


def plane_kernel(small_ref, w_ref, plane_ref, chain_ref):
    ring, rows, _ = small_ref.shape
    columns = rows - EXTRA
    own, half = w_ref.shape[0], ring // 2
    chain_ref[...] = small_ref[:, columns:].astype(F32)[:, 0:1]
    for i in range(plane_ref.shape[0]):
        plane_ref[i, :own] = w_ref[...]
        for j in range(half):
            first = own + j * columns
            plane_ref[i, first : first + columns] = small_ref[(i % 2) * half + j, :columns]


def plane_parts(small, w_head, experts):
    ring, rows, lanes = small.shape
    count = w_head.shape[0] + ring // 2 * (rows - EXTRA)
    return pl.pallas_call(
        plane_kernel,
        out_shape=[
            jax.ShapeDtypeStruct((experts, count, lanes), BF16),
            jax.ShapeDtypeStruct((ring, 1, lanes), F32),
        ],
        in_specs=[vmem_spec()] * 2,
        out_specs=[vmem_spec()] * 2,
        compiler_params=pltpu.CompilerParams(vmem_limit_bytes=60 * MIB),
        cost_estimate=pl.CostEstimate(flops=10**6, bytes_accessed=2 * 10**6, transcendentals=0),
        name="plane_parts",
    )(small, w_head)


def slot_parts(shape, dim, cap):
    slot = lax.broadcasted_iota(jnp.int32, shape, dim)
    return slot // cap, lax.rem(slot, cap)


def pick_kernel(cap, ids_ref, pick_ref):
    topk, tok = ids_ref.shape
    slots = pick_ref.shape[0]
    experts = slots // cap
    named = jnp.zeros((experts, tok), F32)
    sub = lax.broadcasted_iota(jnp.int32, (experts, tok), 0)
    for route in range(topk):
        named = named + jnp.where(ids_ref[route : route + 1, :] == sub, 1.0, 0.0)
    row = lax.broadcasted_iota(jnp.int32, (tok, tok), 0)
    col = lax.broadcasted_iota(jnp.int32, (tok, tok), 1)
    before = jnp.where(row < col, 1.0, 0.0).astype(BF16)
    rank = jnp.dot(named.astype(BF16), before, preferred_element_type=F32)
    mine = jnp.where(named > 0.5, rank, -1.0).astype(BF16)
    expert_of, place_of = slot_parts((slots, experts), 0, cap)
    spread = jnp.where(
        lax.broadcasted_iota(jnp.int32, (slots, experts), 1) == expert_of, 1.0, 0.0
    ).astype(BF16)
    here = jnp.dot(spread, mine, preferred_element_type=F32) == place_of[:, 0:1].astype(F32)
    pick_ref[...] = jnp.where(here, 1.0, 0.0).astype(BF16)


def pick_table(ids, experts, cap):
    tok = ids.shape[0]
    return pl.pallas_call(
        functools.partial(pick_kernel, cap),
        out_shape=jax.ShapeDtypeStruct((experts * cap, tok), BF16),
        in_specs=[vmem_spec()],
        out_specs=vmem_spec(),
        compiler_params=pltpu.CompilerParams(vmem_limit_bytes=8 * MIB),
        cost_estimate=pl.CostEstimate(flops=10**8, bytes_accessed=10**6, transcendentals=0),
        name="pick_table",
    )(ids.T)


def gate_kernel(cap, ids_ref, weights_ref, gate_ref):
    tok, topk = ids_ref.shape
    slots = gate_ref.shape[1]
    experts = slots // cap
    named = jnp.zeros((tok, experts), F32)
    gates = jnp.zeros((tok, experts), F32)
    lane = lax.broadcasted_iota(jnp.int32, (tok, experts), 1)
    for route in range(topk):
        hit = ids_ref[:, route : route + 1] == lane
        named = named + jnp.where(hit, 1.0, 0.0)
        gates = gates + jnp.where(hit, weights_ref[:, route : route + 1], 0.0)
    row = lax.broadcasted_iota(jnp.int32, (tok, tok), 0)
    col = lax.broadcasted_iota(jnp.int32, (tok, tok), 1)
    before = jnp.where(col < row, 1.0, 0.0).astype(BF16)
    rank = jnp.dot(before, named.astype(BF16), preferred_element_type=F32)
    expert_of, place_of = slot_parts((experts, slots), 1, cap)
    spread = jnp.where(
        lax.broadcasted_iota(jnp.int32, (experts, slots), 0) == expert_of, 1.0, 0.0
    ).astype(BF16)
    mine = jnp.where(named > 0.5, rank, -1.0).astype(BF16)
    here = jnp.dot(mine, spread, preferred_element_type=F32) == place_of[0:1, :].astype(F32)
    high = gates.astype(BF16)
    low = (gates - high.astype(F32)).astype(BF16)
    for i, part in enumerate((high, low)):
        wide = jnp.dot(part, spread, preferred_element_type=F32)
        gate_ref[i * tok : (i + 1) * tok] = jnp.where(here, wide, 0.0).astype(BF16)


def gate_tables(ids, weights, experts, cap):
    tok = ids.shape[0]
    return pl.pallas_call(
        functools.partial(gate_kernel, cap),
        out_shape=jax.ShapeDtypeStruct((2 * tok, experts * cap), BF16),
        in_specs=[vmem_spec()] * 2,
        out_specs=vmem_spec(),
        compiler_params=pltpu.CompilerParams(vmem_limit_bytes=8 * MIB),
        cost_estimate=pl.CostEstimate(flops=10**8, bytes_accessed=10**6, transcendentals=0),
        name="gate_tables",
    )(ids, weights)


def attention_kernel(steps, me_ref, bias_ref, chain_ref, w_ref, *refs):
    blocks, (out_ref, w_buf, q_buf, k_buf, v_buf) = refs[:-5], refs[-5:]
    me = me_ref[0]
    ring = len(steps)
    tok = out_ref.shape[1]
    head_dim = out_ref.shape[2]
    width = w_buf.shape[0]
    part = width // w_ref.shape[0]
    for i in range(3):
        w_buf[:, i * head_dim : (i + 1) * head_dim] = w_ref[:, i * part : (i + 1) * part].reshape(
            width, head_dim
        )
    start = 0
    for block in blocks:
        here = slice(start, start + block.shape[0])
        both = jnp.dot(block[...], w_buf[...], preferred_element_type=F32).astype(BF16)
        q_buf[here, :head_dim] = both[:, :head_dim]
        k_buf[here, :head_dim] = both[:, head_dim : 2 * head_dim]
        v_buf[here] = both[:, 2 * head_dim :]
        start += block.shape[0]
    scale = 1.0 / math.sqrt(head_dim)
    lane = lax.broadcasted_iota(jnp.int32, (tok, tok), 1)
    named = jnp.where(lane < 3 * CHAINS, lax.rem(lane, CHAINS), -1).astype(F32)
    whole = jnp.full((tok, tok), bias_ref[me] * math.sqrt(head_dim), F32)
    first = whole.astype(BF16).astype(F32)
    second = (whole - first).astype(BF16).astype(F32)
    third = whole - first - second
    bias = jnp.where(lane < CHAINS, first, jnp.where(lane < 2 * CHAINS, second, third))
    owner = [lax.rem(me + (s + ring), ring) for s in steps]
    for i in range(ring):
        same = jnp.broadcast_to(chain_ref[owner[i]], (tok, tok)).T == named
        here = slice(i * tok, (i + 1) * tok)
        k_buf[here, head_dim:] = jnp.where(same, 1.0, 0.0).astype(BF16)
        q_buf[here, head_dim:] = jnp.where(same, bias, 0.0).astype(BF16)
    count = 4
    for start in range(0, ring, count):
        scores = lax.dot_general(
            q_buf[start * tok : (start + count) * tok],
            k_buf[...],
            (((1,), (1,)), ((), ())),
            preferred_element_type=F32,
        )
        top = jnp.max(scores, axis=-1, keepdims=True)
        raised = jnp.exp2((scores - top) * (scale * math.log2(math.e)))
        probs = (raised * (1.0 / jnp.sum(raised, axis=-1, keepdims=True))).astype(BF16)
        mixed = jnp.dot(probs, v_buf[...], preferred_element_type=F32).astype(BF16)
        for j in range(count):
            out_ref[owner[start + j]] = mixed[j * tok : (j + 1) * tok]


def attention(me, bias, chains, weights, blocks, steps):
    ring = len(steps)
    tok = chains.shape[2]
    head_dim = weights.shape[2]
    width = blocks[0].shape[1]
    length = ring * tok
    return pl.pallas_call(
        functools.partial(attention_kernel, steps),
        out_shape=jax.ShapeDtypeStruct((ring, tok, head_dim), BF16),
        in_specs=[smem_spec(), smem_spec()] + [vmem_spec()] * (2 + len(blocks)),
        out_specs=vmem_spec(),
        scratch_shapes=[
            pltpu.VMEM((width, 3 * head_dim), BF16),
            pltpu.VMEM((length, head_dim + tok), BF16),
            pltpu.VMEM((length, head_dim + tok), BF16),
            pltpu.VMEM((length, head_dim), BF16),
        ],
        compiler_params=pltpu.CompilerParams(vmem_limit_bytes=16 * MIB),
        cost_estimate=pl.CostEstimate(
            flops=1400 * 10**6, bytes_accessed=3 * 10**6, transcendentals=10**6
        ),
        name="attention",
    )(me, bias, chains, weights, *blocks)


def dispatch_kernel(core_ref, heads_ref, *refs):
    parts, refs = refs[:-8], refs[-8:]
    tokens_ref, gain_ref, pick_ref, up_hbm, mixed_ref, out_ref, up_ref, arrived = refs
    copy = pltpu.make_async_copy(up_hbm, up_ref, arrived)
    copy.start()
    core = core_ref[0]
    half = heads_ref.shape[0] // 2
    width = tokens_ref.shape[1]
    mixed = tokens_ref[...].astype(F32)
    for own, side in ((0, core), (half, 1 - core)):
        local = jnp.concatenate([heads_ref[side * half + j] for j in range(half)], axis=1)
        w_out = jnp.concatenate(
            [parts[own + j][...].reshape(width, heads_ref.shape[2]) for j in range(half)], axis=1
        )
        mixed = mixed + lax.dot_general(
            local, w_out, (((1,), (1,)), ((), ())), preferred_element_type=F32
        )
    mixed_ref[...] = mixed
    ffn_in = (
        mixed * lax.rsqrt(jnp.mean(mixed * mixed, axis=-1, keepdims=True) + 1e-05) * gain_ref[...]
    ).astype(BF16)
    out_ref[...] = (
        jnp.dot(pick_ref[...], ffn_in, preferred_element_type=F32)
        .astype(BF16)
        .reshape(out_ref.shape)
    )
    copy.wait()


def dispatch(core, heads, parts, tokens, gain, pick, w_gateup, experts, cap):
    tok, width = tokens.shape
    return pl.pallas_call(
        dispatch_kernel,
        out_shape=[
            jax.ShapeDtypeStruct((tok, width), F32),
            jax.ShapeDtypeStruct((experts, cap, width), BF16),
            jax.ShapeDtypeStruct(w_gateup.shape, BF16),
        ],
        in_specs=[smem_spec()]
        + [vmem_spec()] * (4 + len(parts))
        + [pl.BlockSpec(memory_space=pltpu.HBM)],
        out_specs=[vmem_spec()] * 3,
        scratch_shapes=[pltpu.SemaphoreType.DMA],
        compiler_params=pltpu.CompilerParams(vmem_limit_bytes=40 * MIB),
        cost_estimate=pl.CostEstimate(
            flops=600 * 10**6, bytes_accessed=5 * 10**6, transcendentals=0
        ),
        name="dispatch",
    )(core, heads, *parts, tokens, gain.reshape(1, width), pick, w_gateup)


def expert_kernel(rows_ref, up_ref, down_ref, out_ref):
    hidden = down_ref.shape[0]
    rows = rows_ref[...]
    total = jnp.zeros(rows.shape, F32)
    for first in range(0, hidden, WIDE):
        last = min(first + WIDE, hidden)
        gate = jnp.dot(rows, up_ref[:, first:last], preferred_element_type=F32)
        value = jnp.dot(
            rows, up_ref[:, hidden + first : hidden + last], preferred_element_type=F32
        )
        active = (gate / (1.0 + jnp.exp(-gate)) * value).astype(BF16)
        total = total + jnp.dot(active, down_ref[first:last], preferred_element_type=F32)
    out_ref[...] = total.astype(BF16)


def run_expert(rows, w_gateup, w_down):
    count, width = rows.shape
    hidden = w_down.shape[0]
    return pl.pallas_call(
        expert_kernel,
        out_shape=jax.ShapeDtypeStruct((count, width), BF16),
        in_specs=[vmem_spec()] * 3,
        out_specs=vmem_spec(),
        compiler_params=pltpu.CompilerParams(vmem_limit_bytes=24 * MIB),
        cost_estimate=pl.CostEstimate(
            flops=6 * count * width * hidden, bytes_accessed=9 * 10**6, transcendentals=count * hidden
        ),
        name="experts",
    )(rows, w_gateup, w_down)


def combine_kernel(mixed_ref, gate_ref, back_ref, out_ref):
    tok = mixed_ref.shape[0]
    both = jnp.dot(gate_ref[...], back_ref[...], preferred_element_type=F32)
    out_ref[...] = (mixed_ref[...] + (both[:tok] + both[tok:])).astype(BF16)


def combine(mixed, gates, back):
    return pl.pallas_call(
        combine_kernel,
        out_shape=jax.ShapeDtypeStruct(mixed.shape, BF16),
        in_specs=[vmem_spec()] * 3,
        out_specs=vmem_spec(),
        compiler_params=pltpu.CompilerParams(vmem_limit_bytes=16 * MIB),
        cost_estimate=pl.CostEstimate(
            flops=540 * 10**6, bytes_accessed=4 * 10**6, transcendentals=0
        ),
        name="combine",
    )(mixed, gates, back)


def ring_gather(block, axis):
    size = lax.axis_size(axis)
    up = [(i, (i + 1) % size) for i in range(size)]
    down = [(i, (i - 1) % size) for i in range(size)]
    blocks, steps = [block], [0]
    forth = back = block
    for step in range(1, size // 2):
        forth = lax.ppermute(forth, axis, up)
        back = lax.ppermute(back, axis, down)
        blocks += [forth, back]
        steps += [-step, step]
    half = block.shape[0] // 2
    blocks += [lax.ppermute(forth[:half], axis, up), lax.ppermute(back[half:], axis, down)]
    steps += [size // 2]
    return blocks, steps


def per_device(
    tokens,
    chain_ids,
    route_ids,
    route_weights,
    attn_gain,
    ffn_gain,
    chain_bias,
    w_qkv,
    w_out,
    w_gateup,
    w_down,
):
    inputs = tokens[0]
    tok, width = inputs.shape
    ring = lax.axis_size("ctx")
    experts = lax.axis_size("expert")
    me = lax.axis_index("ctx").astype(jnp.int32).reshape(1)
    core = lax.rem(lax.axis_index("expert").astype(jnp.int32), 2).reshape(1)
    normed, small = start(inputs, attn_gain, w_out, chain_ids, ring)
    blocks, steps = ring_gather(normed, "ctx")

    small = lax.all_to_all(small, "ctx", 0, 0, tiled=True)
    w_head = w_qkv.reshape(-1, w_qkv.shape[2])
    w_head, blocks[1], blocks[2] = lax.optimization_barrier((w_head, blocks[1], blocks[2]))
    parts, chains = plane_parts(small, w_head, experts)
    plane = lax.all_to_all(parts, "expert", 0, 0, tiled=True)
    plane, blocks[-2], blocks[-1] = lax.optimization_barrier((plane, blocks[-2], blocks[-1]))

    mine = w_head.shape[0]
    attended = attention(me, chain_bias, chains, plane[:, :mine], blocks, steps)
    plane, attended = lax.optimization_barrier((plane, attended))
    swap = [(i, i ^ 1) for i in range(experts)]
    rest = plane.shape[1] - mine
    own = [plane[:, mine + i * rest // 4 : mine + (i + 1) * rest // 4] for i in range(4)]
    other = [lax.ppermute(part, "expert", swap) for part in own]
    heads = lax.all_to_all(attended, "ctx", split_axis=0, concat_axis=0, tiled=True)
    pick = pick_table(route_ids[0], experts, CAP)
    gates = gate_tables(route_ids[0], route_weights[0], experts, CAP)
    pick, gates = lax.optimization_barrier((pick, gates))
    mixed, outgoing, w_up = dispatch(
        core, heads, own + other, inputs, ffn_gain, pick, w_gateup[0], experts, CAP
    )
    arrived = lax.all_to_all(outgoing, "expert", split_axis=0, concat_axis=0, tiled=True)
    result = run_expert(arrived.reshape(-1, width), w_up, w_down[0])
    back = lax.all_to_all(
        result.reshape(arrived.shape), "expert", split_axis=0, concat_axis=0, tiled=True
    )
    return combine(mixed, gates, back.reshape(-1, width))[None]


def solution(mesh):
    placed = (
        P("expert", "ctx", None),
        P("expert", "ctx"),
        P("expert", "ctx", None),
        P("expert", "ctx", None),
        P(),
        P(),
        P(),
        P(None, "expert", "ctx"),
        P("ctx", "expert"),
        P("expert", None, None),
        P("expert", None, None),
    )
    return jax.shard_map(
        per_device, mesh=mesh, in_specs=placed, out_specs=P("expert", "ctx", None), check_vma=False
    )
```

```python
import functools
import math

import jax
import jax.numpy as jnp
from jax import lax
from jax.experimental import pallas as pl
from jax.experimental.pallas import tpu as pltpu
from jax.sharding import PartitionSpec as P

F32 = jnp.float32
BF16 = jnp.bfloat16
MIB = 1 << 20
CAP = 32
EXTRA = 48
CHAINS = 8
WIDE = 256
PIECES = 4


def vmem_spec():
    return pl.BlockSpec(memory_space=pltpu.VMEM)


def smem_spec():
    return pl.BlockSpec(memory_space=pltpu.SMEM)


def start_kernel(tokens_ref, gain_ref, w_ref, chain_ref, normed_ref, small_ref):
    wide = tokens_ref[...].astype(F32)
    normed_ref[...] = (
        wide * lax.rsqrt(jnp.mean(wide * wide, axis=-1, keepdims=True) + 1e-05) * gain_ref[...]
    ).astype(BF16)
    columns = w_ref.shape[0]
    chains = jnp.broadcast_to(chain_ref[...].astype(F32), (EXTRA, w_ref.shape[1])).astype(BF16)
    for i in range(small_ref.shape[0]):
        small_ref[i, :columns] = w_ref[...]
        small_ref[i, columns:] = chains


def start(tokens, gain, w_out, chain_ids, ring):
    tok, width = tokens.shape
    columns = w_out.shape[1]
    return pl.pallas_call(
        start_kernel,
        out_shape=[
            jax.ShapeDtypeStruct((tok, width), BF16),
            jax.ShapeDtypeStruct((ring, columns + EXTRA, tok), BF16),
        ],
        in_specs=[vmem_spec()] * 4,
        out_specs=[vmem_spec()] * 2,
        compiler_params=pltpu.CompilerParams(vmem_limit_bytes=60 * MIB),
        cost_estimate=pl.CostEstimate(flops=10**6, bytes_accessed=10**6, transcendentals=0),
        name="start",
    )(tokens, gain.reshape(1, width), w_out.T, chain_ids)


def plane_kernel(small_ref, w_ref, plane_ref, chain_ref):
    ring, rows, _ = small_ref.shape
    columns = rows - EXTRA
    own, half = w_ref.shape[0], ring // 2
    chain_ref[...] = small_ref[:, columns:].astype(F32)[:, 0:1]
    for i in range(plane_ref.shape[0]):
        plane_ref[i, :own] = w_ref[...]
        for j in range(half):
            first = own + j * columns
            plane_ref[i, first : first + columns] = small_ref[(i % 2) * half + j, :columns]


def plane_parts(small, w_head, experts):
    ring, rows, lanes = small.shape
    count = w_head.shape[0] + ring // 2 * (rows - EXTRA)
    return pl.pallas_call(
        plane_kernel,
        out_shape=[
            jax.ShapeDtypeStruct((experts, count, lanes), BF16),
            jax.ShapeDtypeStruct((ring, 1, lanes), F32),
        ],
        in_specs=[vmem_spec()] * 2,
        out_specs=[vmem_spec()] * 2,
        compiler_params=pltpu.CompilerParams(vmem_limit_bytes=40 * MIB),
        cost_estimate=pl.CostEstimate(flops=10**6, bytes_accessed=2 * 10**6, transcendentals=0),
        name="plane_parts",
    )(small, w_head)


def slot_parts(shape, dim, cap):
    slot = lax.broadcasted_iota(jnp.int32, shape, dim)
    return slot // cap, lax.rem(slot, cap)


def pick_kernel(cap, ids_ref, pick_ref):
    topk, tok = ids_ref.shape
    slots = pick_ref.shape[0]
    experts = slots // cap
    named = jnp.zeros((experts, tok), F32)
    sub = lax.broadcasted_iota(jnp.int32, (experts, tok), 0)
    for route in range(topk):
        named = named + jnp.where(ids_ref[route : route + 1, :] == sub, 1.0, 0.0)
    row = lax.broadcasted_iota(jnp.int32, (tok, tok), 0)
    col = lax.broadcasted_iota(jnp.int32, (tok, tok), 1)
    before = jnp.where(row < col, 1.0, 0.0).astype(BF16)
    rank = jnp.dot(named.astype(BF16), before, preferred_element_type=F32)
    mine = jnp.where(named > 0.5, rank, -1.0).astype(BF16)
    expert_of, place_of = slot_parts((slots, experts), 0, cap)
    spread = jnp.where(
        lax.broadcasted_iota(jnp.int32, (slots, experts), 1) == expert_of, 1.0, 0.0
    ).astype(BF16)
    here = jnp.dot(spread, mine, preferred_element_type=F32) == place_of[:, 0:1].astype(F32)
    pick_ref[...] = jnp.where(here, 1.0, 0.0).astype(BF16)


def pick_table(ids, experts, cap):
    tok = ids.shape[0]
    return pl.pallas_call(
        functools.partial(pick_kernel, cap),
        out_shape=jax.ShapeDtypeStruct((experts * cap, tok), BF16),
        in_specs=[vmem_spec()],
        out_specs=vmem_spec(),
        compiler_params=pltpu.CompilerParams(vmem_limit_bytes=8 * MIB),
        cost_estimate=pl.CostEstimate(flops=10**8, bytes_accessed=10**6, transcendentals=0),
        name="pick_table",
    )(ids.T)


def gate_kernel(cap, ids_ref, weights_ref, gate_ref):
    tok, topk = ids_ref.shape
    slots = gate_ref.shape[1]
    experts = slots // cap
    named = jnp.zeros((tok, experts), F32)
    gates = jnp.zeros((tok, experts), F32)
    lane = lax.broadcasted_iota(jnp.int32, (tok, experts), 1)
    for route in range(topk):
        hit = ids_ref[:, route : route + 1] == lane
        named = named + jnp.where(hit, 1.0, 0.0)
        gates = gates + jnp.where(hit, weights_ref[:, route : route + 1], 0.0)
    row = lax.broadcasted_iota(jnp.int32, (tok, tok), 0)
    col = lax.broadcasted_iota(jnp.int32, (tok, tok), 1)
    before = jnp.where(col < row, 1.0, 0.0).astype(BF16)
    rank = jnp.dot(before, named.astype(BF16), preferred_element_type=F32)
    expert_of, place_of = slot_parts((experts, slots), 1, cap)
    spread = jnp.where(
        lax.broadcasted_iota(jnp.int32, (experts, slots), 0) == expert_of, 1.0, 0.0
    ).astype(BF16)
    mine = jnp.where(named > 0.5, rank, -1.0).astype(BF16)
    here = jnp.dot(mine, spread, preferred_element_type=F32) == place_of[0:1, :].astype(F32)
    high = gates.astype(BF16)
    low = (gates - high.astype(F32)).astype(BF16)
    for i, part in enumerate((high, low)):
        wide = jnp.dot(part, spread, preferred_element_type=F32)
        gate_ref[i * tok : (i + 1) * tok] = jnp.where(here, wide, 0.0).astype(BF16)


def gate_tables(ids, weights, experts, cap):
    tok = ids.shape[0]
    return pl.pallas_call(
        functools.partial(gate_kernel, cap),
        out_shape=jax.ShapeDtypeStruct((2 * tok, experts * cap), BF16),
        in_specs=[vmem_spec()] * 2,
        out_specs=vmem_spec(),
        compiler_params=pltpu.CompilerParams(vmem_limit_bytes=8 * MIB),
        cost_estimate=pl.CostEstimate(flops=10**8, bytes_accessed=10**6, transcendentals=0),
        name="gate_tables",
    )(ids, weights)


def attention_kernel(steps, me_ref, bias_ref, chain_ref, w_ref, *refs):
    blocks, (out_ref, w_buf, q_buf, k_buf, v_buf) = refs[:-5], refs[-5:]
    me = me_ref[0]
    ring = len(steps)
    tok = out_ref.shape[1]
    head_dim = out_ref.shape[2]
    width = w_buf.shape[0]
    part = width // w_ref.shape[0]
    for i in range(3):
        w_buf[:, i * head_dim : (i + 1) * head_dim] = w_ref[:, i * part : (i + 1) * part].reshape(
            width, head_dim
        )
    start = 0
    for block in blocks:
        here = slice(start, start + block.shape[0])
        both = jnp.dot(block[...], w_buf[...], preferred_element_type=F32).astype(BF16)
        q_buf[here, :head_dim] = both[:, :head_dim]
        k_buf[here, :head_dim] = both[:, head_dim : 2 * head_dim]
        v_buf[here] = both[:, 2 * head_dim :]
        start += block.shape[0]
    scale = 1.0 / math.sqrt(head_dim)
    lane = lax.broadcasted_iota(jnp.int32, (tok, tok), 1)
    named = jnp.where(lane < 3 * CHAINS, lax.rem(lane, CHAINS), -1).astype(F32)
    whole = jnp.full((tok, tok), bias_ref[me] * math.sqrt(head_dim), F32)
    first = whole.astype(BF16).astype(F32)
    second = (whole - first).astype(BF16).astype(F32)
    third = whole - first - second
    bias = jnp.where(lane < CHAINS, first, jnp.where(lane < 2 * CHAINS, second, third))
    owner = [lax.rem(me + (s + ring), ring) for s in steps]
    for i in range(ring):
        same = jnp.broadcast_to(chain_ref[owner[i]], (tok, tok)).T == named
        here = slice(i * tok, (i + 1) * tok)
        k_buf[here, head_dim:] = jnp.where(same, 1.0, 0.0).astype(BF16)
        q_buf[here, head_dim:] = jnp.where(same, bias, 0.0).astype(BF16)
    count = 4
    for start in range(0, ring, count):
        scores = lax.dot_general(
            q_buf[start * tok : (start + count) * tok],
            k_buf[...],
            (((1,), (1,)), ((), ())),
            preferred_element_type=F32,
        )
        top = jnp.max(scores, axis=-1, keepdims=True)
        raised = jnp.exp2((scores - top) * (scale * math.log2(math.e)))
        probs = (raised * (1.0 / jnp.sum(raised, axis=-1, keepdims=True))).astype(BF16)
        mixed = jnp.dot(probs, v_buf[...], preferred_element_type=F32).astype(BF16)
        for j in range(count):
            out_ref[owner[start + j]] = mixed[j * tok : (j + 1) * tok]


def attention(me, bias, chains, weights, blocks, steps):
    ring = len(steps)
    tok = chains.shape[2]
    head_dim = weights.shape[2]
    width = blocks[0].shape[1]
    length = ring * tok
    return pl.pallas_call(
        functools.partial(attention_kernel, steps),
        out_shape=jax.ShapeDtypeStruct((ring, tok, head_dim), BF16),
        in_specs=[smem_spec(), smem_spec()] + [vmem_spec()] * (2 + len(blocks)),
        out_specs=vmem_spec(),
        scratch_shapes=[
            pltpu.VMEM((width, 3 * head_dim), BF16),
            pltpu.VMEM((length, head_dim + tok), BF16),
            pltpu.VMEM((length, head_dim + tok), BF16),
            pltpu.VMEM((length, head_dim), BF16),
        ],
        compiler_params=pltpu.CompilerParams(vmem_limit_bytes=16 * MIB),
        cost_estimate=pl.CostEstimate(
            flops=1400 * 10**6, bytes_accessed=3 * 10**6, transcendentals=10**6
        ),
        name="attention",
    )(me, bias, chains, weights, *blocks)


def dispatch_kernel(core_ref, heads_ref, *refs):
    parts, refs = refs[:-8], refs[-8:]
    tokens_ref, gain_ref, pick_ref, up_hbm, mixed_ref, out_ref, up_ref, arrived = refs
    rows = up_hbm.shape[0] // PIECES
    copies = []
    for i in range(PIECES):
        here = pl.ds(i * rows, rows)
        copies.append(pltpu.make_async_copy(up_hbm.at[here], up_ref.at[here], arrived.at[i]))
        copies[-1].start()
    core = core_ref[0]
    half = heads_ref.shape[0] // 2
    width = tokens_ref.shape[1]
    mixed = tokens_ref[...].astype(F32)
    for own, side in ((0, core), (half, 1 - core)):
        local = jnp.concatenate([heads_ref[side * half + j] for j in range(half)], axis=1)
        w_out = jnp.concatenate(
            [parts[own + j][...].reshape(width, heads_ref.shape[2]) for j in range(half)], axis=1
        )
        mixed = mixed + lax.dot_general(
            local, w_out, (((1,), (1,)), ((), ())), preferred_element_type=F32
        )
    mixed_ref[...] = mixed
    ffn_in = (
        mixed * lax.rsqrt(jnp.mean(mixed * mixed, axis=-1, keepdims=True) + 1e-05) * gain_ref[...]
    ).astype(BF16)
    out_ref[...] = (
        jnp.dot(pick_ref[...], ffn_in, preferred_element_type=F32)
        .astype(BF16)
        .reshape(out_ref.shape)
    )
    for copy in copies:
        copy.wait()


def dispatch(core, heads, parts, tokens, gain, pick, w_gateup, experts, cap):
    tok, width = tokens.shape
    return pl.pallas_call(
        dispatch_kernel,
        out_shape=[
            jax.ShapeDtypeStruct((tok, width), F32),
            jax.ShapeDtypeStruct((experts, cap, width), BF16),
            jax.ShapeDtypeStruct(w_gateup.shape, BF16),
        ],
        in_specs=[smem_spec()]
        + [vmem_spec()] * (4 + len(parts))
        + [pl.BlockSpec(memory_space=pltpu.HBM)],
        out_specs=[vmem_spec()] * 3,
        scratch_shapes=[pltpu.SemaphoreType.DMA((PIECES,))],
        compiler_params=pltpu.CompilerParams(vmem_limit_bytes=40 * MIB),
        cost_estimate=pl.CostEstimate(
            flops=600 * 10**6, bytes_accessed=5 * 10**6, transcendentals=0
        ),
        name="dispatch",
    )(core, heads, *parts, tokens, gain.reshape(1, width), pick, w_gateup)


def expert_kernel(rows_ref, up_ref, down_ref, out_ref):
    hidden = down_ref.shape[0]
    rows = rows_ref[...]
    total = jnp.zeros(rows.shape, F32)
    for first in range(0, hidden, WIDE):
        last = min(first + WIDE, hidden)
        gate = jnp.dot(rows, up_ref[:, first:last], preferred_element_type=F32)
        value = jnp.dot(
            rows, up_ref[:, hidden + first : hidden + last], preferred_element_type=F32
        )
        active = (gate / (1.0 + jnp.exp(-gate)) * value).astype(BF16)
        total = total + jnp.dot(active, down_ref[first:last], preferred_element_type=F32)
    out_ref[...] = total.astype(BF16)


def run_expert(rows, w_gateup, w_down):
    count, width = rows.shape
    hidden = w_down.shape[0]
    return pl.pallas_call(
        expert_kernel,
        out_shape=jax.ShapeDtypeStruct((count, width), BF16),
        in_specs=[vmem_spec()] * 3,
        out_specs=vmem_spec(),
        compiler_params=pltpu.CompilerParams(vmem_limit_bytes=24 * MIB),
        cost_estimate=pl.CostEstimate(
            flops=6 * count * width * hidden, bytes_accessed=9 * 10**6, transcendentals=count * hidden
        ),
        name="experts",
    )(rows, w_gateup, w_down)


def combine_kernel(mixed_ref, gate_ref, back_ref, out_ref):
    tok = mixed_ref.shape[0]
    both = jnp.dot(gate_ref[...], back_ref[...], preferred_element_type=F32)
    out_ref[...] = (mixed_ref[...] + (both[:tok] + both[tok:])).astype(BF16)


def combine(mixed, gates, back):
    return pl.pallas_call(
        combine_kernel,
        out_shape=jax.ShapeDtypeStruct(mixed.shape, BF16),
        in_specs=[vmem_spec()] * 3,
        out_specs=vmem_spec(),
        compiler_params=pltpu.CompilerParams(vmem_limit_bytes=16 * MIB),
        cost_estimate=pl.CostEstimate(
            flops=540 * 10**6, bytes_accessed=4 * 10**6, transcendentals=0
        ),
        name="combine",
    )(mixed, gates, back)


def ring_gather(block, axis):
    size = lax.axis_size(axis)
    up = [(i, (i + 1) % size) for i in range(size)]
    down = [(i, (i - 1) % size) for i in range(size)]
    blocks, steps = [block], [0]
    forth = back = block
    for step in range(1, size // 2):
        forth = lax.ppermute(forth, axis, up)
        back = lax.ppermute(back, axis, down)
        blocks += [forth, back]
        steps += [-step, step]
    half = block.shape[0] // 2
    blocks += [lax.ppermute(forth[:half], axis, up), lax.ppermute(back[half:], axis, down)]
    steps += [size // 2]
    return blocks, steps


def per_device(
    tokens,
    chain_ids,
    route_ids,
    route_weights,
    attn_gain,
    ffn_gain,
    chain_bias,
    w_qkv,
    w_out,
    w_gateup,
    w_down,
):
    inputs = tokens[0]
    tok, width = inputs.shape
    ring = lax.axis_size("ctx")
    experts = lax.axis_size("expert")
    me = lax.axis_index("ctx").astype(jnp.int32).reshape(1)
    core = lax.rem(lax.axis_index("expert").astype(jnp.int32), 2).reshape(1)
    normed, small = start(inputs, attn_gain, w_out, chain_ids, ring)
    blocks, steps = ring_gather(normed, "ctx")

    small = lax.all_to_all(small, "ctx", 0, 0, tiled=True)
    w_head = w_qkv.reshape(-1, w_qkv.shape[2])
    w_head, blocks[1], blocks[2] = lax.optimization_barrier((w_head, blocks[1], blocks[2]))
    parts, chains = plane_parts(small, w_head, experts)
    plane = lax.all_to_all(parts, "expert", 0, 0, tiled=True)
    plane, blocks[-2], blocks[-1] = lax.optimization_barrier((plane, blocks[-2], blocks[-1]))

    mine = w_head.shape[0]
    attended = attention(me, chain_bias, chains, plane[:, :mine], blocks, steps)
    plane, attended = lax.optimization_barrier((plane, attended))
    swap = [(i, i ^ 1) for i in range(experts)]
    rest = plane.shape[1] - mine
    own = [plane[:, mine + i * rest // 4 : mine + (i + 1) * rest // 4] for i in range(4)]
    other = [lax.ppermute(part, "expert", swap) for part in own]
    heads = lax.all_to_all(attended, "ctx", split_axis=0, concat_axis=0, tiled=True)
    pick = pick_table(route_ids[0], experts, CAP)
    gates = gate_tables(route_ids[0], route_weights[0], experts, CAP)
    pick, gates = lax.optimization_barrier((pick, gates))
    mixed, outgoing, w_up = dispatch(
        core, heads, own + other, inputs, ffn_gain, pick, w_gateup[0], experts, CAP
    )
    arrived = lax.all_to_all(outgoing, "expert", split_axis=0, concat_axis=0, tiled=True)
    result = run_expert(arrived.reshape(-1, width), w_up, w_down[0])
    back = lax.all_to_all(
        result.reshape(arrived.shape), "expert", split_axis=0, concat_axis=0, tiled=True
    )
    return combine(mixed, gates, back.reshape(-1, width))[None]


def solution(mesh):
    placed = (
        P("expert", "ctx", None),
        P("expert", "ctx"),
        P("expert", "ctx", None),
        P("expert", "ctx", None),
        P(),
        P(),
        P(),
        P(None, "expert", "ctx"),
        P("ctx", "expert"),
        P("expert", None, None),
        P("expert", None, None),
    )
    return jax.shard_map(
        per_device, mesh=mesh, in_specs=placed, out_specs=P("expert", "ctx", None), check_vma=False
    )
```

```python
import functools
import math

import jax
import jax.numpy as jnp
from jax import lax
from jax.experimental import pallas as pl
from jax.experimental.pallas import tpu as pltpu
from jax.sharding import PartitionSpec as P

F32 = jnp.float32
BF16 = jnp.bfloat16
MIB = 1 << 20
CAP = 32
EXTRA = 16
CHAINS = 8
WIDE = 256


def vmem_spec():
    return pl.BlockSpec(memory_space=pltpu.VMEM)


def smem_spec():
    return pl.BlockSpec(memory_space=pltpu.SMEM)


def start_kernel(tokens_ref, gain_ref, w_ref, chain_ref, normed_ref, small_ref):
    wide = tokens_ref[...].astype(F32)
    normed_ref[...] = (
        wide * lax.rsqrt(jnp.mean(wide * wide, axis=-1, keepdims=True) + 1e-05) * gain_ref[...]
    ).astype(BF16)
    columns = w_ref.shape[0]
    chains = jnp.broadcast_to(chain_ref[...].astype(F32), (EXTRA, w_ref.shape[1])).astype(BF16)
    for i in range(small_ref.shape[0]):
        small_ref[i, :columns] = w_ref[...]
        small_ref[i, columns:] = chains


def start(tokens, gain, w_out, chain_ids, ring):
    tok, width = tokens.shape
    columns = w_out.shape[1]
    return pl.pallas_call(
        start_kernel,
        out_shape=[
            jax.ShapeDtypeStruct((tok, width), BF16),
            jax.ShapeDtypeStruct((ring, columns + EXTRA, tok), BF16),
        ],
        in_specs=[vmem_spec()] * 4,
        out_specs=[vmem_spec()] * 2,
        compiler_params=pltpu.CompilerParams(vmem_limit_bytes=60 * MIB),
        cost_estimate=pl.CostEstimate(flops=10**6, bytes_accessed=10**6, transcendentals=0),
        name="start",
    )(tokens, gain.reshape(1, width), w_out.T, chain_ids)


def plane_kernel(small_ref, w_ref, plane_ref, chain_ref):
    ring, rows, _ = small_ref.shape
    columns = rows - EXTRA
    own, half = w_ref.shape[0], ring // 2
    chain_ref[...] = small_ref[:, columns:].astype(F32)[:, 0:1]
    for i in range(plane_ref.shape[0]):
        plane_ref[i, :own] = w_ref[...]
        for j in range(half):
            first = own + j * columns
            plane_ref[i, first : first + columns] = small_ref[(i % 2) * half + j, :columns]


def plane_parts(small, w_head, experts):
    ring, rows, lanes = small.shape
    count = w_head.shape[0] + ring // 2 * (rows - EXTRA)
    return pl.pallas_call(
        plane_kernel,
        out_shape=[
            jax.ShapeDtypeStruct((experts, count, lanes), BF16),
            jax.ShapeDtypeStruct((ring, 1, lanes), F32),
        ],
        in_specs=[vmem_spec()] * 2,
        out_specs=[vmem_spec()] * 2,
        compiler_params=pltpu.CompilerParams(vmem_limit_bytes=40 * MIB),
        cost_estimate=pl.CostEstimate(flops=10**6, bytes_accessed=2 * 10**6, transcendentals=0),
        name="plane_parts",
    )(small, w_head)


def slot_parts(shape, dim, cap):
    slot = lax.broadcasted_iota(jnp.int32, shape, dim)
    return slot // cap, lax.rem(slot, cap)


def pick_kernel(cap, ids_ref, pick_ref):
    topk, tok = ids_ref.shape
    slots = pick_ref.shape[0]
    experts = slots // cap
    named = jnp.zeros((experts, tok), F32)
    sub = lax.broadcasted_iota(jnp.int32, (experts, tok), 0)
    for route in range(topk):
        named = named + jnp.where(ids_ref[route : route + 1, :] == sub, 1.0, 0.0)
    row = lax.broadcasted_iota(jnp.int32, (tok, tok), 0)
    col = lax.broadcasted_iota(jnp.int32, (tok, tok), 1)
    before = jnp.where(row < col, 1.0, 0.0).astype(BF16)
    rank = jnp.dot(named.astype(BF16), before, preferred_element_type=F32)
    mine = jnp.where(named > 0.5, rank, -1.0).astype(BF16)
    expert_of, place_of = slot_parts((slots, experts), 0, cap)
    spread = jnp.where(
        lax.broadcasted_iota(jnp.int32, (slots, experts), 1) == expert_of, 1.0, 0.0
    ).astype(BF16)
    here = jnp.dot(spread, mine, preferred_element_type=F32) == place_of[:, 0:1].astype(F32)
    pick_ref[...] = jnp.where(here, 1.0, 0.0).astype(BF16)


def pick_table(ids, experts, cap):
    tok = ids.shape[0]
    return pl.pallas_call(
        functools.partial(pick_kernel, cap),
        out_shape=jax.ShapeDtypeStruct((experts * cap, tok), BF16),
        in_specs=[vmem_spec()],
        out_specs=vmem_spec(),
        compiler_params=pltpu.CompilerParams(vmem_limit_bytes=8 * MIB),
        cost_estimate=pl.CostEstimate(flops=10**8, bytes_accessed=10**6, transcendentals=0),
        name="pick_table",
    )(ids.T)


def gate_kernel(cap, ids_ref, weights_ref, gate_ref):
    tok, topk = ids_ref.shape
    slots = gate_ref.shape[1]
    experts = slots // cap
    named = jnp.zeros((tok, experts), F32)
    gates = jnp.zeros((tok, experts), F32)
    lane = lax.broadcasted_iota(jnp.int32, (tok, experts), 1)
    for route in range(topk):
        hit = ids_ref[:, route : route + 1] == lane
        named = named + jnp.where(hit, 1.0, 0.0)
        gates = gates + jnp.where(hit, weights_ref[:, route : route + 1], 0.0)
    row = lax.broadcasted_iota(jnp.int32, (tok, tok), 0)
    col = lax.broadcasted_iota(jnp.int32, (tok, tok), 1)
    before = jnp.where(col < row, 1.0, 0.0).astype(BF16)
    rank = jnp.dot(before, named.astype(BF16), preferred_element_type=F32)
    expert_of, place_of = slot_parts((experts, slots), 1, cap)
    spread = jnp.where(
        lax.broadcasted_iota(jnp.int32, (experts, slots), 0) == expert_of, 1.0, 0.0
    ).astype(BF16)
    mine = jnp.where(named > 0.5, rank, -1.0).astype(BF16)
    here = jnp.dot(mine, spread, preferred_element_type=F32) == place_of[0:1, :].astype(F32)
    high = gates.astype(BF16)
    low = (gates - high.astype(F32)).astype(BF16)
    for i, part in enumerate((high, low)):
        wide = jnp.dot(part, spread, preferred_element_type=F32)
        gate_ref[i * tok : (i + 1) * tok] = jnp.where(here, wide, 0.0).astype(BF16)


def gate_tables(ids, weights, experts, cap):
    tok = ids.shape[0]
    return pl.pallas_call(
        functools.partial(gate_kernel, cap),
        out_shape=jax.ShapeDtypeStruct((2 * tok, experts * cap), BF16),
        in_specs=[vmem_spec()] * 2,
        out_specs=vmem_spec(),
        compiler_params=pltpu.CompilerParams(vmem_limit_bytes=8 * MIB),
        cost_estimate=pl.CostEstimate(flops=10**8, bytes_accessed=10**6, transcendentals=0),
        name="gate_tables",
    )(ids, weights)


def attention_kernel(steps, me_ref, bias_ref, chain_ref, w_ref, *refs):
    blocks, (out_ref, w_buf, q_buf, k_buf, v_buf) = refs[:-5], refs[-5:]
    me = me_ref[0]
    ring = len(steps)
    tok = out_ref.shape[1]
    head_dim = out_ref.shape[2]
    width = w_buf.shape[0]
    part = width // w_ref.shape[0]
    for i in range(3):
        w_buf[:, i * head_dim : (i + 1) * head_dim] = w_ref[:, i * part : (i + 1) * part].reshape(
            width, head_dim
        )
    start = 0
    for block in blocks:
        here = slice(start, start + block.shape[0])
        both = jnp.dot(block[...], w_buf[...], preferred_element_type=F32).astype(BF16)
        q_buf[here, :head_dim] = both[:, :head_dim]
        k_buf[here, :head_dim] = both[:, head_dim : 2 * head_dim]
        v_buf[here] = both[:, 2 * head_dim :]
        start += block.shape[0]
    scale = 1.0 / math.sqrt(head_dim)
    lane = lax.broadcasted_iota(jnp.int32, (tok, tok), 1)
    named = jnp.where(lane < 3 * CHAINS, lax.rem(lane, CHAINS), -1).astype(F32)
    whole = jnp.full((tok, tok), bias_ref[me] * math.sqrt(head_dim), F32)
    first = whole.astype(BF16).astype(F32)
    second = (whole - first).astype(BF16).astype(F32)
    third = whole - first - second
    bias = jnp.where(lane < CHAINS, first, jnp.where(lane < 2 * CHAINS, second, third))
    owner = [lax.rem(me + (s + ring), ring) for s in steps]
    for i in range(ring):
        same = jnp.broadcast_to(chain_ref[owner[i]], (tok, tok)).T == named
        here = slice(i * tok, (i + 1) * tok)
        k_buf[here, head_dim:] = jnp.where(same, 1.0, 0.0).astype(BF16)
        q_buf[here, head_dim:] = jnp.where(same, bias, 0.0).astype(BF16)
    count = 4
    for start in range(0, ring, count):
        scores = lax.dot_general(
            q_buf[start * tok : (start + count) * tok],
            k_buf[...],
            (((1,), (1,)), ((), ())),
            preferred_element_type=F32,
        )
        top = jnp.max(scores, axis=-1, keepdims=True)
        raised = jnp.exp2((scores - top) * (scale * math.log2(math.e)))
        probs = (raised * (1.0 / jnp.sum(raised, axis=-1, keepdims=True))).astype(BF16)
        mixed = jnp.dot(probs, v_buf[...], preferred_element_type=F32).astype(BF16)
        for j in range(count):
            out_ref[owner[start + j]] = mixed[j * tok : (j + 1) * tok]


def attention(me, bias, chains, weights, blocks, steps):
    ring = len(steps)
    tok = chains.shape[2]
    head_dim = weights.shape[2]
    width = blocks[0].shape[1]
    length = ring * tok
    return pl.pallas_call(
        functools.partial(attention_kernel, steps),
        out_shape=jax.ShapeDtypeStruct((ring, tok, head_dim), BF16),
        in_specs=[smem_spec(), smem_spec()] + [vmem_spec()] * (2 + len(blocks)),
        out_specs=vmem_spec(),
        scratch_shapes=[
            pltpu.VMEM((width, 3 * head_dim), BF16),
            pltpu.VMEM((length, head_dim + tok), BF16),
            pltpu.VMEM((length, head_dim + tok), BF16),
            pltpu.VMEM((length, head_dim), BF16),
        ],
        compiler_params=pltpu.CompilerParams(vmem_limit_bytes=16 * MIB),
        cost_estimate=pl.CostEstimate(
            flops=1400 * 10**6, bytes_accessed=3 * 10**6, transcendentals=10**6
        ),
        name="attention",
    )(me, bias, chains, weights, *blocks)


def dispatch_kernel(core_ref, heads_ref, *refs):
    parts, refs = refs[:-8], refs[-8:]
    tokens_ref, gain_ref, pick_ref, up_hbm, mixed_ref, out_ref, up_ref, arrived = refs
    copy = pltpu.make_async_copy(up_hbm, up_ref, arrived)
    copy.start()
    core = core_ref[0]
    half = heads_ref.shape[0] // 2
    width = tokens_ref.shape[1]
    mixed = tokens_ref[...].astype(F32)
    for own, side in ((0, core), (half, 1 - core)):
        local = jnp.concatenate([heads_ref[side * half + j] for j in range(half)], axis=1)
        w_out = jnp.concatenate(
            [parts[own + j][...].reshape(width, heads_ref.shape[2]) for j in range(half)], axis=1
        )
        mixed = mixed + lax.dot_general(
            local, w_out, (((1,), (1,)), ((), ())), preferred_element_type=F32
        )
    mixed_ref[...] = mixed
    ffn_in = (
        mixed * lax.rsqrt(jnp.mean(mixed * mixed, axis=-1, keepdims=True) + 1e-05) * gain_ref[...]
    ).astype(BF16)
    out_ref[...] = (
        jnp.dot(pick_ref[...], ffn_in, preferred_element_type=F32)
        .astype(BF16)
        .reshape(out_ref.shape)
    )
    copy.wait()


def dispatch(core, heads, parts, tokens, gain, pick, w_gateup, experts, cap):
    tok, width = tokens.shape
    return pl.pallas_call(
        dispatch_kernel,
        out_shape=[
            jax.ShapeDtypeStruct((tok, width), F32),
            jax.ShapeDtypeStruct((experts, cap, width), BF16),
            jax.ShapeDtypeStruct(w_gateup.shape, BF16),
        ],
        in_specs=[smem_spec()]
        + [vmem_spec()] * (4 + len(parts))
        + [pl.BlockSpec(memory_space=pltpu.HBM)],
        out_specs=[vmem_spec()] * 3,
        scratch_shapes=[pltpu.SemaphoreType.DMA],
        compiler_params=pltpu.CompilerParams(vmem_limit_bytes=40 * MIB),
        cost_estimate=pl.CostEstimate(
            flops=600 * 10**6, bytes_accessed=5 * 10**6, transcendentals=0
        ),
        name="dispatch",
    )(core, heads, *parts, tokens, gain.reshape(1, width), pick, w_gateup)


def expert_kernel(rows_ref, up_ref, down_ref, out_ref):
    hidden = down_ref.shape[0]
    rows = rows_ref[...]
    total = jnp.zeros(rows.shape, F32)
    for first in range(0, hidden, WIDE):
        last = min(first + WIDE, hidden)
        gate = jnp.dot(rows, up_ref[:, first:last], preferred_element_type=F32)
        value = jnp.dot(
            rows, up_ref[:, hidden + first : hidden + last], preferred_element_type=F32
        )
        active = (gate / (1.0 + jnp.exp(-gate)) * value).astype(BF16)
        total = total + jnp.dot(active, down_ref[first:last], preferred_element_type=F32)
    out_ref[...] = total.astype(BF16)


def run_expert(rows, w_gateup, w_down):
    count, width = rows.shape
    hidden = w_down.shape[0]
    return pl.pallas_call(
        expert_kernel,
        out_shape=jax.ShapeDtypeStruct((count, width), BF16),
        in_specs=[vmem_spec()] * 3,
        out_specs=vmem_spec(),
        compiler_params=pltpu.CompilerParams(vmem_limit_bytes=24 * MIB),
        cost_estimate=pl.CostEstimate(
            flops=6 * count * width * hidden, bytes_accessed=9 * 10**6, transcendentals=count * hidden
        ),
        name="experts",
    )(rows, w_gateup, w_down)


def combine_kernel(mixed_ref, gate_ref, back_ref, out_ref):
    tok = mixed_ref.shape[0]
    both = jnp.dot(gate_ref[...], back_ref[...], preferred_element_type=F32)
    out_ref[...] = (mixed_ref[...] + (both[:tok] + both[tok:])).astype(BF16)


def combine(mixed, gates, back):
    return pl.pallas_call(
        combine_kernel,
        out_shape=jax.ShapeDtypeStruct(mixed.shape, BF16),
        in_specs=[vmem_spec()] * 3,
        out_specs=vmem_spec(),
        compiler_params=pltpu.CompilerParams(vmem_limit_bytes=16 * MIB),
        cost_estimate=pl.CostEstimate(
            flops=540 * 10**6, bytes_accessed=4 * 10**6, transcendentals=0
        ),
        name="combine",
    )(mixed, gates, back)


def ring_gather(block, axis):
    size = lax.axis_size(axis)
    up = [(i, (i + 1) % size) for i in range(size)]
    down = [(i, (i - 1) % size) for i in range(size)]
    blocks, steps = [block], [0]
    forth = back = block
    for step in range(1, size // 2):
        forth = lax.ppermute(forth, axis, up)
        back = lax.ppermute(back, axis, down)
        blocks += [forth, back]
        steps += [-step, step]
    half = block.shape[0] // 2
    blocks += [lax.ppermute(forth[:half], axis, up), lax.ppermute(back[half:], axis, down)]
    steps += [size // 2]
    return blocks, steps


def per_device(
    tokens,
    chain_ids,
    route_ids,
    route_weights,
    attn_gain,
    ffn_gain,
    chain_bias,
    w_qkv,
    w_out,
    w_gateup,
    w_down,
):
    inputs = tokens[0]
    tok, width = inputs.shape
    ring = lax.axis_size("ctx")
    experts = lax.axis_size("expert")
    me = lax.axis_index("ctx").astype(jnp.int32).reshape(1)
    core = lax.rem(lax.axis_index("expert").astype(jnp.int32), 2).reshape(1)
    normed, small = start(inputs, attn_gain, w_out, chain_ids, ring)
    blocks, steps = ring_gather(normed, "ctx")

    small = lax.all_to_all(small, "ctx", 0, 0, tiled=True)
    w_head = w_qkv.reshape(-1, w_qkv.shape[2])
    w_head, blocks[1], blocks[2] = lax.optimization_barrier((w_head, blocks[1], blocks[2]))
    parts, chains = plane_parts(small, w_head, experts)
    plane = lax.all_to_all(parts, "expert", 0, 0, tiled=True)
    plane, blocks[-2], blocks[-1] = lax.optimization_barrier((plane, blocks[-2], blocks[-1]))

    mine = w_head.shape[0]
    attended = attention(me, chain_bias, chains, plane[:, :mine], blocks, steps)
    plane, attended = lax.optimization_barrier((plane, attended))
    swap = [(i, i ^ 1) for i in range(experts)]
    rest = plane.shape[1] - mine
    own = [plane[:, mine + i * rest // 4 : mine + (i + 1) * rest // 4] for i in range(4)]
    other = [lax.ppermute(part, "expert", swap) for part in own]
    heads = lax.all_to_all(attended, "ctx", split_axis=0, concat_axis=0, tiled=True)
    pick = pick_table(route_ids[0], experts, CAP)
    gates = gate_tables(route_ids[0], route_weights[0], experts, CAP)
    pick, gates = lax.optimization_barrier((pick, gates))
    mixed, outgoing, w_up = dispatch(
        core, heads, own + other, inputs, ffn_gain, pick, w_gateup[0], experts, CAP
    )
    arrived = lax.all_to_all(outgoing, "expert", split_axis=0, concat_axis=0, tiled=True)
    result = run_expert(arrived.reshape(-1, width), w_up, w_down[0])
    back = lax.all_to_all(
        result.reshape(arrived.shape), "expert", split_axis=0, concat_axis=0, tiled=True
    )
    return combine(mixed, gates, back.reshape(-1, width))[None]


def solution(mesh):
    placed = (
        P("expert", "ctx", None),
        P("expert", "ctx"),
        P("expert", "ctx", None),
        P("expert", "ctx", None),
        P(),
        P(),
        P(),
        P(None, "expert", "ctx"),
        P("ctx", "expert"),
        P("expert", None, None),
        P("expert", None, None),
    )
    return jax.shard_map(
        per_device, mesh=mesh, in_specs=placed, out_specs=P("expert", "ctx", None), check_vma=False
    )
```
